256 devices in a mesh: fsdp: 64 (over z_lo, y, x, core), dp: 4 (over z_hi).
Axes of the slice: x: 4, y: 4, z: 8 (z_hi: 4, z_lo: 2; z = z_hi * 2 + z_lo), core: 2. Of those that a mesh axis runs over, the one named last changes fastest.
Arguments:
- inputs: bfloat16 [4, 8192, 2560], P('dp', 'fsdp'), may hold values from -16 to 16
- up_weight: bfloat16 [2560, 6912], P('fsdp', 'dp'), may hold values from -0.125 to 0.125
- out_grad: bfloat16 [4, 8192, 6912], P(None, 'fsdp', 'dp'), may hold values from -6 to 6
Outputs:
- outputs: bfloat16 [4, 8192, 6912], P(None, 'fsdp', 'dp')
- in_grad: bfloat16 [4, 8192, 2560], P('dp', 'fsdp')
- up_grad: float32 [2560, 6912], P('fsdp', 'dp')
The draws below stay inside these ranges and needn't reach their ends.
All inputs are finite; a program needn't handle non-finite values.
Results may differ from the reference program's by a relative error of at most 0.013.
Values may be sent and summed in bfloat16 or wider, within the bound.
A program may use at most 128 MiB of HBM per device.

```python
import jax
import jax.numpy as jnp
from jax import lax

D = 2560
F = 6912
SEQ = 8192
CLIPS = 4
GROUPS = 4


def spiked(result, own_key, source, target, parts, factor):
    def block_of(axis_at):
        return (jnp.arange(result.shape[axis_at]) // (result.shape[axis_at] // parts)).reshape((-1,) + (1,) * (result.ndim - 1 - axis_at))

    first = jax.random.permutation(own_key, parts)[block_of(target)]
    far = (block_of(target) + parts // 2) % parts
    return jnp.where((block_of(source) == first) | (block_of(source) == far), factor * result, result)


def block_scale(stream_key, dims, cuts, low, top_value):
    loudness = 1.0
    for dim, parts in cuts:
        draws = jax.random.uniform(jax.random.fold_in(jax.random.fold_in(stream_key, 6), dim), (parts,), jnp.float32, low / len(cuts), top_value / len(cuts))
        loudness = loudness * jnp.repeat(jnp.exp(draws), dims[dim] // parts).reshape((-1,) + (1,) * (len(dims) - 1 - dim))
    return loudness


def centred(key, dims, deviation, reach, shards=(), held_as=jnp.bfloat16):
    gain = block_scale(key, dims, shards, -0.22, 0.18) if shards else 1.0
    entries = jax.random.normal(key, dims, jnp.float32) * deviation * gain
    return jnp.minimum(jnp.maximum(entries, -reach), reach).astype(held_as)


def gaussian_with(key, extent, scale, reach, cuts, heavy, dtype=jnp.bfloat16):
    drawn = scale * jax.random.normal(key, extent, jnp.float32)
    if cuts:
        drawn = drawn * block_scale(key, extent, cuts, -0.22, 0.18)
    return jnp.clip(spiked(drawn, jax.random.fold_in(key, 3), *heavy), -reach, reach).astype(dtype)


def setup_inputs(seed: int = 0) -> dict:
    keys = jax.random.split(jax.random.key(seed), 4)
    return {
        "inputs": gaussian_with(keys[0], (CLIPS, SEQ, D), 1.0, 16.0, ((0, 4), (1, 64)), (1, 2, 64, 4.0)),
        "up_weight": centred(keys[1], (D, F), D ** -0.5, 0.125, ((0, 64), (1, 4))),
        "out_grad": centred(keys[2], (CLIPS, SEQ, F), 1.0, 6.0, ((1, 64), (2, 4))),
    }


def gelu_tanh(value):
    return jax.nn.gelu(value, approximate=True)

def reference(inputs, up_weight, out_grad):
    tok_rows = inputs.reshape(CLIPS * SEQ, D)
    grad_rows = out_grad.reshape(CLIPS * SEQ, F)
    pre = jnp.dot(tok_rows, up_weight, preferred_element_type=jnp.float32)
    outputs = gelu_tanh(pre).astype(jnp.bfloat16)
    pre_grad = jax.vjp(gelu_tanh, pre)[1](grad_rows.astype(jnp.float32))[0].astype(jnp.bfloat16)
    block_width = F // GROUPS
    in_total = jnp.zeros((CLIPS * SEQ, D), jnp.float32)
    for block in range(GROUPS):
        low = block * block_width
        part = jnp.dot(pre_grad[:, low:low + block_width], up_weight[:, low:low + block_width].T, preferred_element_type=jnp.float32)
        rounded = lax.optimization_barrier(part.astype(jnp.bfloat16))
        in_total = in_total + rounded.astype(jnp.float32)
    in_grad = in_total.astype(jnp.bfloat16)
    factor = 1.0 / jnp.sqrt(jnp.float32(CLIPS * SEQ))
    up_grad = jnp.dot(tok_rows.T, pre_grad, preferred_element_type=jnp.float32) * factor
    return (outputs.reshape(CLIPS, SEQ, F), in_grad.reshape(CLIPS, SEQ, D), up_grad)
```

```python
import functools

import jax
import jax.numpy as jnp
from jax import lax
from jax.experimental import pallas as pl
from jax.experimental.pallas import tpu as pltpu
from jax.sharding import PartitionSpec as P

MESH = pl.DeviceIdType.MESH
F32, BF16 = jnp.float32, jnp.bfloat16
SIDE = 4
TILE = 256
CHUNK = 64


def place(device):
    return {"fsdp": device[0], "dp": device[1]}


def remote(src, dst, send_sem, recv_sem, device):
    return pltpu.make_async_remote_copy(
        src_ref=src, dst_ref=dst, send_sem=send_sem, recv_sem=recv_sem,
        device_id=place(device), device_id_type=MESH,
    )


def gelu_pair(v):
    c = 0.7978845608028654
    sq = v * v
    t = jnp.tanh(v * (c + (c * 0.044715) * sq))
    half = 0.5 * (1.0 + t)
    slope = half + (0.5 * v) * (1.0 - t * t) * (c + (3.0 * c * 0.044715) * sq)
    return v * half, slope


def kernel(
    factor, x_hbm, w_ref, gt_hbm, out_hbm, ing_hbm, dw_ref,
    xall, xt, wfull, wst, gt, g, pg, outn, outt, pre, psend, zr1, zr2, ing,
    lhs, ssend, srecv, dsend, r1, r2, r3, d4, r4, fin,
    send_sem, w_sem, x_sem, z1_sem, z2_sem, s_sem, r_sem, local_sem,
):
    fs, p = lax.axis_index("fsdp"), lax.axis_index("dp")
    k = lax.rem(fs, 2)
    x = lax.rem(lax.div(fs, 2), SIDE)
    y = lax.rem(lax.div(fs, 2 * SIDE), SIDE)
    l = lax.div(fs, 2 * SIDE * SIDE)
    home = k == l
    a = x * (1 - k) + y * k
    b = y * (1 - k) + x * k
    toks = xall.shape[1]
    half_toks = toks // 2
    rows = wfull.shape[2]
    width = wfull.shape[3]
    units = w_ref.shape[1]
    tiles = width // TILE
    quarter = psend.shape[3]
    quarters = psend.shape[0]

    def m4(v):
        return lax.rem(v, SIDE)

    def device(a_to, b_to):
        x_to = a_to * (1 - k) + b_to * k
        y_to = b_to * (1 - k) + a_to * k
        return (((l * SIDE + y_to) * SIDE + x_to) * 2 + k, p)

    def flat(h, a_at, b_at):
        return (a_at * (1 - h) + b_at * h) + SIDE * (b_at * (1 - h) + a_at * h)

    sibling = (fs + 1 - 2 * k, p)
    across = (fs + (1 - 2 * l) * (2 * SIDE * SIDE), p)
    a_next, a_prev, a_far = (device(m4(a + i), b) for i in (1, 3, 2))
    b_next, b_prev = device(a, m4(b + 1)), device(a, m4(b + 3))
    p_next, p_prev, p_far = m4(p + 1), m4(p + 3), m4(p + 2)
    dp_next, dp_prev = (fs, p_next), (fs, p_prev)

    sends = []

    def push(src, dst, recv_sem, to):
        copy = remote(src, dst, send_sem.at[len(sends)], recv_sem, to)
        sends.append(copy)
        copy.start()

    def arrive(dst, recv_sem):
        remote(dst, dst, send_sem.at[0], recv_sem, sibling).wait_recv()

    load_x = pltpu.make_async_copy(x_hbm.at[0], xall.at[p], local_sem.at[0])
    load_x.start()
    load_g = pltpu.make_async_copy(gt_hbm, gt.at[:, pl.ds(0, units), :], local_sem.at[1])
    load_g.start()

    barrier = pltpu.get_barrier_semaphore()
    peers = (sibling, across, a_next, a_prev, a_far, b_next, b_prev, dp_next, dp_prev)
    for peer in peers:
        pl.semaphore_signal(barrier, inc=1, device_id=place(peer), device_id_type=MESH)

    wst[k] = jnp.zeros(wst.shape[1:], F32)
    wst[k, :, pl.ds(0, units)] = w_ref[...].astype(F32)
    gt[:, pl.ds(units, width - units), :] = jnp.zeros((SIDE, width - units, toks), BF16)
    load_x.wait()
    pl.semaphore_wait(barrier, len(peers))

    mine = flat(k, a, b)

    def wblock(h, at):
        return wfull.at[h, at]

    def wsem(h, at):
        return w_sem.at[h * (SIDE * SIDE) + at]

    stage = remote(wst.at[k], wst.at[k], send_sem.at[send_sem.shape[0] - 1], s_sem.at[4], sibling)

    @pl.when(jnp.logical_not(home))
    def _():
        stage.start()

    lo, hi = pl.ds(0, half_toks), pl.ds(half_toks, half_toks)
    push(xall.at[p, lo], xall.at[p, lo], x_sem.at[0], dp_next)
    push(xall.at[p, hi], xall.at[p, hi], x_sem.at[2], dp_prev)
    push(xall.at[p, hi], xall.at[p, hi], x_sem.at[1], dp_next)
    push(xall.at[p, lo], xall.at[p, lo], x_sem.at[3], dp_prev)

    cross = remote(
        wblock(k, mine), wblock(k, mine), send_sem.at[send_sem.shape[0] - 2], wsem(k, mine), across
    )

    @pl.when(home)
    def _():
        arrive(wst.at[1 - k], s_sem.at[4])
        wfull[k, mine] = wst[...].reshape(rows, width).astype(BF16)
        cross.start()

    @pl.when(jnp.logical_not(home))
    def _():
        arrive(wblock(k, mine), wsem(k, mine))

    def share(at, *devices):
        for to in devices:
            push(wblock(k, at), wblock(k, at), wsem(k, at), to)

    order = (0, 1, 3, 2)
    by_next = (0, 3)
    share(mine, a_next, a_prev, a_far, b_next, b_prev, sibling)
    for i in order[1:]:
        at = flat(k, m4(a + i), b)
        arrive(wblock(k, at), wsem(k, at))
        share(at, b_next, b_prev, sibling)

    arrive(xall.at[p_prev, lo], x_sem.at[0])
    push(xall.at[p_prev, lo], xall.at[p_prev, lo], x_sem.at[4], dp_next)
    arrive(xall.at[p_next, hi], x_sem.at[2])
    push(xall.at[p_next, hi], xall.at[p_next, hi], x_sem.at[5], dp_prev)

    load_g.wait()

    def turn_g(step, _):
        clip, j = lax.div(step, tiles), lax.rem(step, tiles)
        at = pl.ds(pl.multiple_of(j * TILE, TILE), TILE)
        block = gt[clip, at, :].astype(F32).T.astype(BF16)
        g[pl.ds(pl.multiple_of(clip * toks, toks), toks), at] = block
        return 0

    lax.fori_loop(0, SIDE * tiles, turn_g, 0)

    for i in order:
        at = flat(k, m4(a + i), m4(b + 3))
        arrive(wblock(k, at), wsem(k, at))
        share(at, *((b_next, sibling) if i in by_next else (sibling,)))
        at = flat(k, m4(a + i), m4(b + 1))
        arrive(wblock(k, at), wsem(k, at))
        share(at, *((sibling,) if i in by_next else (b_prev, sibling)))
    for i in order:
        at = flat(k, m4(a + i), m4(b + 2))
        arrive(wblock(k, at), wsem(k, at))
        share(at, sibling)
    for at in range(SIDE * SIDE):
        arrive(wblock(1 - k, at), wsem(1 - k, at))
    arrive(xall.at[p_prev, hi], x_sem.at[1])
    arrive(xall.at[p_next, lo], x_sem.at[3])
    arrive(xall.at[p_far, lo], x_sem.at[4])
    arrive(xall.at[p_far, hi], x_sem.at[5])

    def forward(j, _):
        at = pl.ds(pl.multiple_of(j * TILE, TILE), TILE)
        pre[...] = jnp.dot(
            xall[...].reshape(SIDE * toks, -1), wfull[:, :, :, at].reshape(-1, TILE), preferred_element_type=F32
        )

        def chunk(r, _):
            span = pl.ds(pl.multiple_of(r * CHUNK, CHUNK), CHUNK)
            value, slope = gelu_pair(pre[span, :])
            outn[span, at] = value.astype(BF16)
            pg[span, at] = (g[span, at].astype(F32) * slope).astype(BF16)
            return 0

        lax.fori_loop(0, SIDE * toks // CHUNK, chunk, 0)
        return 0

    lax.fori_loop(0, tiles, forward, 0)

    blocks = quarter // rows
    for q in range(quarters):
        first = q * blocks
        h, at = first // (SIDE * SIDE), first % (SIDE * SIDE)
        wq = wfull[h, pl.ds(at, blocks)].reshape(quarter, width)
        part = lax.dot_general(pg[...], wq, (((1,), (1,)), ((), ())), preferred_element_type=F32)
        psend[q] = part.astype(BF16).reshape(SIDE, toks, quarter)
        push(psend.at[q, p_far, lo], zr1.at[q, 0], z1_sem.at[2 * q], dp_next)
        push(psend.at[q, p_far, hi], zr1.at[q, 1], z1_sem.at[2 * q + 1], dp_prev)

    def merge(q):
        arrive(zr1.at[q, 0], z1_sem.at[2 * q])
        psend[q, p_next, lo] = (psend[q, p_next, lo].astype(F32) + zr1[q, 0].astype(F32)).astype(BF16)
        push(psend.at[q, p_next], zr2.at[q, 0], z2_sem.at[2 * q], dp_next)
        arrive(zr1.at[q, 1], z1_sem.at[2 * q + 1])
        psend[q, p_prev, hi] = (psend[q, p_prev, hi].astype(F32) + zr1[q, 1].astype(F32)).astype(BF16)
        push(psend.at[q, p_prev], zr2.at[q, 1], z2_sem.at[2 * q + 1], dp_prev)

    def turn_x(clip, _):
        at = pl.ds(pl.multiple_of(clip * toks, toks), toks)
        for q in range(quarters):
            first = q * blocks
            h, here = first // (SIDE * SIDE), first % (SIDE * SIDE)
            block = xall[clip, :, pl.ds(q * quarter, quarter)].astype(F32).T.astype(BF16)
            xt[h, pl.ds(here, blocks), :, at] = block.reshape(blocks, rows, toks)
        return 0

    lax.fori_loop(0, SIDE, turn_x, 0)

    def slab(h, s, store):
        for i in range(SIDE):
            lhs[pl.ds(i * rows, rows), :] = xt[h, flat(h, i, s)]

        def step(j, _):
            at = pl.ds(pl.multiple_of(j * TILE, TILE), TILE)
            store(at, jnp.dot(lhs[...], pg[:, at], preferred_element_type=F32).reshape(SIDE, rows, TILE))
            return 0

        lax.fori_loop(0, tiles, step, 0)

    for n, i in enumerate((2, 1, 3, 0)):
        s = m4(a + i)

        def to_sibling(at, value):
            ssend[s, :, :, at] = value.astype(BF16)

        slab(1 - k, s, to_sibling)
        push(ssend.at[s], srecv.at[s], s_sem.at[n], sibling)
        merge(n)

    for n, i in enumerate((2, 1, 3, 0)):
        s = m4(b + i)
        arrive(srecv.at[s], s_sem.at[n])
        if i == 1:
            arrive(r1.at[0], r_sem.at[0])
        if i == 3:
            arrive(r1.at[1], r_sem.at[1])

        def keep(at, value):
            total = value + srecv[s, :, :, at].astype(F32)
            if i == 1:
                total = jnp.concatenate([total[:2] + r1[0, :, :, at].astype(F32), total[2:]], axis=0)
            if i == 3:
                total = jnp.concatenate([total[:2], total[2:] + r1[1, :, :, at].astype(F32)], axis=0)
            dsend[s, :, :, at] = total.astype(BF16)

        slab(k, s, keep)
        if i == 2:
            push(dsend.at[s, pl.ds(0, 2)], r1.at[0], r_sem.at[0], b_next)
            push(dsend.at[s, pl.ds(2, 2)], r1.at[1], r_sem.at[1], b_prev)
        if i == 1:
            push(dsend.at[s], r2.at[0], r_sem.at[2], b_next)
        if i == 3:
            push(dsend.at[s], r2.at[1], r_sem.at[3], b_prev)

    def turn_out(step, _):
        clip, j = lax.div(step, tiles), lax.rem(step, tiles)
        at = pl.ds(pl.multiple_of(j * TILE, TILE), TILE)
        block = outn[pl.ds(pl.multiple_of(clip * toks, toks), toks), at].astype(F32).T.astype(BF16)
        outt[clip, at, :] = block
        return 0

    lax.fori_loop(0, SIDE * tiles, turn_out, 0)
    store_out = pltpu.make_async_copy(outt.at[:, pl.ds(0, units), :], out_hbm, local_sem.at[1])
    store_out.start()

    arrive(r2.at[0], r_sem.at[2])
    arrive(r2.at[1], r_sem.at[3])
    for i, to in ((2, a_far), (1, a_next), (3, a_prev), (0, None)):
        ai = m4(a + i)

        def gathered(j, _):
            at = pl.ds(pl.multiple_of(j * TILE, TILE), TILE)
            total = dsend[b, ai, :, at].astype(F32) + r2[0, ai, :, at].astype(F32) + r2[1, ai, :, at].astype(F32)
            dsend[b, ai, :, at] = total.astype(BF16)
            return 0

        lax.fori_loop(0, tiles, gathered, 0)
        if to is not None:
            push(dsend.at[b, ai], r3.at[i - 1], r_sem.at[3 + i], to)

    for q in range(quarters):
        arrive(zr2.at[q, 0], z2_sem.at[2 * q])
        arrive(zr2.at[q, 1], z2_sem.at[2 * q + 1])
        total = psend[q, p].astype(F32) + zr2[q, 0].astype(F32) + zr2[q, 1].astype(F32)
        ing[:, pl.ds(q * quarter, quarter)] = total.astype(BF16)
    store_ing = pltpu.make_async_copy(ing, ing_hbm.at[0], local_sem.at[0])
    store_ing.start()

    for i in (1, 2, 3):
        arrive(r3.at[i - 1], r_sem.at[3 + i])

    def plane(at):
        return dsend[b, a, :, at].astype(F32) + sum(r3[i, :, at].astype(F32) for i in range(3))

    last = remote(d4, r4, send_sem.at[send_sem.shape[0] - 3], r_sem.at[7], across)
    back = remote(fin.at[1 - k], fin.at[1 - k], send_sem.at[send_sem.shape[0] - 4], s_sem.at[5], sibling)

    @pl.when(jnp.logical_not(home))
    def _():
        def step(j, _):
            at = pl.ds(pl.multiple_of(j * TILE, TILE), TILE)
            d4[:, at] = plane(at).astype(BF16)
            return 0

        lax.fori_loop(0, tiles, step, 0)
        last.start()
        last.wait_send()
        arrive(fin.at[k], s_sem.at[5])

    @pl.when(home)
    def _():
        arrive(r4, r_sem.at[7])

        def step(j, _):
            at = pl.ds(pl.multiple_of(j * TILE, TILE), TILE)
            fin[:, :, at] = ((plane(at) + r4[:, at].astype(F32)) * factor).reshape(2, rows // 2, TILE)
            return 0

        lax.fori_loop(0, tiles, step, 0)
        back.start()
        back.wait_send()

    dw_ref[...] = fin[k, :, pl.ds(0, units)]

    @pl.when(home)
    def _():
        cross.wait_send()

    @pl.when(jnp.logical_not(home))
    def _():
        stage.wait_send()

    for copy in sends:
        copy.wait_send()
    store_out.wait()
    store_ing.wait()


def on_device(inputs, up_weight, out_grad):
    _, toks, depth = inputs.shape
    own_rows, units = up_weight.shape
    clips = out_grad.shape[0]
    rows = 2 * own_rows
    chips = SIDE * SIDE
    width = -(-units // TILE) * TILE
    quarters = 4
    quarter = depth // quarters
    every = clips * toks
    factor = 1.0 / float(every * 4 * chips) ** 0.5

    out_t, in_grad, up_grad = pl.pallas_call(
        functools.partial(kernel, factor),
        out_shape=(
            jax.ShapeDtypeStruct((clips, units, toks), BF16),
            jax.ShapeDtypeStruct((1, toks, depth), BF16),
            jax.ShapeDtypeStruct((own_rows, units), F32),
        ),
        in_specs=[
            pl.BlockSpec(memory_space=pl.ANY),
            pl.BlockSpec(memory_space=pltpu.VMEM),
            pl.BlockSpec(memory_space=pl.ANY),
        ],
        out_specs=(
            pl.BlockSpec(memory_space=pl.ANY),
            pl.BlockSpec(memory_space=pl.ANY),
            pl.BlockSpec(memory_space=pltpu.VMEM),
        ),
        scratch_shapes=[
            pltpu.VMEM((clips, toks, depth), BF16),
            pltpu.VMEM((2, chips, rows, every), BF16),
            pltpu.VMEM((2, chips, rows, width), BF16),
            pltpu.VMEM((2, own_rows, width), F32),
            pltpu.VMEM((clips, width, toks), BF16),
            pltpu.VMEM((every, width), BF16),
            pltpu.VMEM((every, width), BF16),
            pltpu.VMEM((every, width), BF16),
            pltpu.VMEM((clips, width, toks), BF16),
            pltpu.VMEM((every, TILE), F32),
            pltpu.VMEM((quarters, clips, toks, quarter), BF16),
            pltpu.VMEM((quarters, 2, toks // 2, quarter), BF16),
            pltpu.VMEM((quarters, 2, toks, quarter), BF16),
            pltpu.VMEM((toks, depth), BF16),
            pltpu.VMEM((SIDE * rows, every), BF16),
            pltpu.VMEM((SIDE, SIDE, rows, width), BF16),
            pltpu.VMEM((SIDE, SIDE, rows, width), BF16),
            pltpu.VMEM((SIDE, SIDE, rows, width), BF16),
            pltpu.VMEM((2, 2, rows, width), BF16),
            pltpu.VMEM((2, SIDE, rows, width), BF16),
            pltpu.VMEM((3, rows, width), BF16),
            pltpu.VMEM((rows, width), BF16),
            pltpu.VMEM((rows, width), BF16),
            pltpu.VMEM((2, own_rows, width), F32),
            pltpu.SemaphoreType.DMA((72,)),
            pltpu.SemaphoreType.DMA((2 * chips,)),
            pltpu.SemaphoreType.DMA((6,)),
            pltpu.SemaphoreType.DMA((2 * quarters,)),
            pltpu.SemaphoreType.DMA((2 * quarters,)),
            pltpu.SemaphoreType.DMA((6,)),
            pltpu.SemaphoreType.DMA((8,)),
            pltpu.SemaphoreType.DMA((2,)),
        ],
        compiler_params=pltpu.CompilerParams(
            collective_id=0, has_side_effects=True, vmem_limit_bytes=60 * 1024 * 1024
        ),
        cost_estimate=pl.CostEstimate(
            flops=6 * every * depth * units, bytes_accessed=6_000_000, transcendentals=every * units
        ),
    )(inputs, up_weight, out_grad.transpose(0, 2, 1))
    return out_t.transpose(0, 2, 1), in_grad, up_grad


def solution(mesh):
    in_specs = (P("dp", "fsdp", None), P("fsdp", "dp"), P(None, "fsdp", "dp"))
    out_specs = (P(None, "fsdp", "dp"), P("dp", "fsdp", None), P("fsdp", "dp"))
    return jax.shard_map(
        on_device, mesh=mesh, in_specs=in_specs, out_specs=out_specs, check_vma=False
    )
```

```python
import functools

import jax
import jax.numpy as jnp
from jax import lax
from jax.experimental import pallas as pl
from jax.experimental.pallas import tpu as pltpu
from jax.sharding import PartitionSpec as P

MESH = pl.DeviceIdType.MESH
F32, BF16 = jnp.float32, jnp.bfloat16
SIDE = 4
TILE = 256
CHUNK = 64


def place(device):
    return {"fsdp": device[0], "dp": device[1]}


def remote(src, dst, send_sem, recv_sem, device):
    return pltpu.make_async_remote_copy(
        src_ref=src, dst_ref=dst, send_sem=send_sem, recv_sem=recv_sem,
        device_id=place(device), device_id_type=MESH,
    )


def gelu_pair(v):
    c = 0.7978845608028654
    sq = v * v
    t = jnp.tanh(v * (c + (c * 0.044715) * sq))
    half = 0.5 * (1.0 + t)
    slope = half + (0.5 * v) * (1.0 - t * t) * (c + (3.0 * c * 0.044715) * sq)
    return v * half, slope


def kernel(
    factor, x_hbm, w_ref, gt_hbm, out_hbm, ing_hbm, dw_ref,
    xall, xt, wfull, wown, wst, gt, g, pg, outn, outt, pre, psend, zr1, zr2, ing,
    lhs, ssend, srecv, dsend, r1, r2, r3, d4, r4, fin,
    send_sem, w_sem, p_sem, x_sem, z1_sem, z2_sem, s_sem, r_sem, local_sem,
):
    fs, p = lax.axis_index("fsdp"), lax.axis_index("dp")
    k = lax.rem(fs, 2)
    x = lax.rem(lax.div(fs, 2), SIDE)
    y = lax.rem(lax.div(fs, 2 * SIDE), SIDE)
    l = lax.div(fs, 2 * SIDE * SIDE)
    home = k == l
    a = x * (1 - k) + y * k
    b = y * (1 - k) + x * k
    toks = xall.shape[1]
    half_toks = toks // 2
    near = (SIDE - 1) * toks
    rows = wfull.shape[2]
    own_rows = rows // 2
    width = wfull.shape[3]
    units = w_ref.shape[1]
    tiles = width // TILE
    quarter = psend.shape[3]
    quarters = psend.shape[0]
    blocks = quarter // rows

    def m4(v):
        return lax.rem(v, SIDE)

    def device(a_to, b_to):
        x_to = a_to * (1 - k) + b_to * k
        y_to = b_to * (1 - k) + a_to * k
        return (((l * SIDE + y_to) * SIDE + x_to) * 2 + k, p)

    def flat(h, a_at, b_at):
        return (a_at * (1 - h) + b_at * h) + SIDE * (b_at * (1 - h) + a_at * h)

    def clip_at(slot):
        return m4(p + jnp.where(slot == 0, 0, jnp.where(slot == 1, 3, slot - 1)))

    sibling = (fs + 1 - 2 * k, p)
    across = (fs + (1 - 2 * l) * (2 * SIDE * SIDE), p)
    askew = (across[0] + 1 - 2 * k, p)
    a_next, a_prev, a_far = (device(m4(a + i), b) for i in (1, 3, 2))
    b_next, b_prev = device(a, m4(b + 1)), device(a, m4(b + 3))
    dp_next, dp_prev = (fs, m4(p + 1)), (fs, m4(p + 3))

    sends = []

    def push(src, dst, recv_sem, to):
        copy = remote(src, dst, send_sem.at[len(sends)], recv_sem, to)
        sends.append(copy)
        copy.start()

    def arrive(dst, recv_sem):
        remote(dst, dst, send_sem.at[0], recv_sem, sibling).wait_recv()

    load_x = pltpu.make_async_copy(x_hbm.at[0], xall.at[0], local_sem.at[0])
    load_x.start()
    load_g = pltpu.make_async_copy(gt_hbm, gt.at[:, pl.ds(0, units), :], local_sem.at[1])
    load_g.start()

    barrier = pltpu.get_barrier_semaphore()
    peers = (sibling, across, askew, a_next, a_prev, a_far, b_next, b_prev, dp_next, dp_prev)
    for peer in peers:
        pl.semaphore_signal(barrier, inc=1, device_id=place(peer), device_id_type=MESH)

    spare = wown.shape[0] - own_rows
    wown[:, pl.ds(units, width - units)] = jnp.zeros((wown.shape[0], width - units), BF16)
    wown[:, pl.ds(0, units)] = jnp.concatenate([w_ref[...].astype(F32), jnp.zeros((spare, units), F32)], axis=0).astype(BF16)

    @pl.when(home)
    def _():
        wst[k] = wown[...]

    gt[:, pl.ds(units, width - units), :] = jnp.zeros((SIDE, width - units, toks), BF16)
    load_x.wait()
    pl.semaphore_wait(barrier, len(peers))

    mine = flat(k, a, b)

    def wblock(h, at):
        return wfull.at[h, at]

    def wsem(h, at):
        return w_sem.at[h * (SIDE * SIDE) + at]

    stage = remote(wown, wst.at[k], send_sem.at[send_sem.shape[0] - 1], p_sem.at[k], sibling)
    cross = remote(wown, wst.at[k], send_sem.at[send_sem.shape[0] - 2], p_sem.at[k], (across[0] + l - k, p))
    cross.start()

    @pl.when(jnp.logical_not(home))
    def _():
        stage.start()

    lo, hi = pl.ds(0, half_toks), pl.ds(half_toks, half_toks)
    push(xall.at[0, lo], xall.at[1, lo], x_sem.at[0], dp_next)
    push(xall.at[0, hi], xall.at[2, hi], x_sem.at[2], dp_prev)

    arrive(wst.at[1 - k], p_sem.at[1 - k])

    @pl.when(jnp.logical_not(home))
    def _():
        arrive(wst.at[k], p_sem.at[k])

    wfull[k, mine] = wst[...].astype(F32)[:, :own_rows].reshape(rows, width).astype(BF16)

    def share(at, *devices):
        for to in devices:
            push(wblock(k, at), wblock(k, at), wsem(k, at), to)

    order = (0, 1, 3, 2)
    by_next = (0, 3)
    share(mine, a_next, a_prev, a_far, b_next, b_prev, sibling)

    load_g.wait()

    def turn_g(step, _):
        slot, j = lax.div(step, tiles), lax.rem(step, tiles)
        at = pl.ds(pl.multiple_of(j * TILE, TILE), TILE)
        block = gt[clip_at(slot), at, :].astype(F32).T.astype(BF16)
        g[pl.ds(pl.multiple_of(slot * toks, toks), toks), at] = block
        return 0

    lax.fori_loop(0, SIDE * tiles, turn_g, 0)

    push(xall.at[0, hi], xall.at[1, hi], x_sem.at[1], dp_next)
    push(xall.at[0, lo], xall.at[2, lo], x_sem.at[3], dp_prev)
    for i in order[1:]:
        at = flat(k, m4(a + i), b)
        arrive(wblock(k, at), wsem(k, at))
        share(at, b_next, b_prev, sibling)

    arrive(xall.at[1, lo], x_sem.at[0])
    push(xall.at[1, lo], xall.at[3, lo], x_sem.at[4], dp_next)
    arrive(xall.at[2, hi], x_sem.at[2])
    push(xall.at[2, hi], xall.at[3, hi], x_sem.at[5], dp_prev)

    for i in order:
        at = flat(k, m4(a + i), m4(b + 3))
        arrive(wblock(k, at), wsem(k, at))
        share(at, *((b_next, sibling) if i in by_next else (sibling,)))
        at = flat(k, m4(a + i), m4(b + 1))
        arrive(wblock(k, at), wsem(k, at))
        share(at, *((sibling,) if i in by_next else (b_prev, sibling)))

    def turn_x(slot, _):
        at = pl.ds(pl.multiple_of(slot * toks, toks), toks)
        for q in range(quarters):
            first = q * blocks
            h, here = first // (SIDE * SIDE), first % (SIDE * SIDE)
            block = xall[slot, :, pl.ds(q * quarter, quarter)].astype(F32).T.astype(BF16)
            xt[h, pl.ds(here, blocks), :, at] = block.reshape(blocks, rows, toks)
        return 0

    arrive(xall.at[1, hi], x_sem.at[1])
    arrive(xall.at[2, lo], x_sem.at[3])
    lax.fori_loop(0, SIDE - 1, turn_x, 0)

    for i in order:
        at = flat(k, m4(a + i), m4(b + 2))
        arrive(wblock(k, at), wsem(k, at))
        share(at, sibling)
    for at in range(SIDE * SIDE):
        arrive(wblock(1 - k, at), wsem(1 - k, at))

    def forward(first, count):
        def tile(j, _):
            at = pl.ds(pl.multiple_of(j * TILE, TILE), TILE)
            pre[pl.ds(0, count * toks), :] = jnp.dot(
                xall[pl.ds(first, count)].reshape(count * toks, -1),
                wfull[:, :, :, at].reshape(-1, TILE), preferred_element_type=F32,
            )

            def chunk(r, _):
                span = pl.ds(pl.multiple_of(r * CHUNK, CHUNK), CHUNK)
                to = pl.ds(pl.multiple_of(r * CHUNK + first * toks, CHUNK), CHUNK)
                value, slope = gelu_pair(pre[span, :])
                outn[to, at] = value.astype(BF16)
                pg[to, at] = (g[to, at].astype(F32) * slope).astype(BF16)
                return 0

            lax.fori_loop(0, count * toks // CHUNK, chunk, 0)
            return 0

        lax.fori_loop(0, tiles, tile, 0)

    def in_grad_part(q, first, count):
        start = q * blocks
        h, at = start // (SIDE * SIDE), start % (SIDE * SIDE)
        wq = wfull[h, pl.ds(at, blocks)].reshape(quarter, width)
        part = lax.dot_general(
            pg[pl.ds(first * toks, count * toks), :], wq, (((1,), (1,)), ((), ())), preferred_element_type=F32
        )
        psend[q, pl.ds(first, count)] = part.astype(BF16).reshape(count, toks, quarter)

    forward(0, SIDE - 1)

    for q in range(quarters):
        in_grad_part(q, 0, SIDE - 1)
        push(psend.at[q, 2, hi], zr2.at[q, 0, hi], z2_sem.at[4 * q], dp_next)
        push(psend.at[q, 1, lo], zr2.at[q, 1, lo], z2_sem.at[4 * q + 1], dp_prev)

    arrive(xall.at[3, lo], x_sem.at[4])
    arrive(xall.at[3, hi], x_sem.at[5])
    forward(SIDE - 1, 1)

    for q in range(quarters):
        in_grad_part(q, SIDE - 1, 1)
        push(psend.at[q, 3, lo], zr1.at[q, 0], z1_sem.at[2 * q], dp_next)
        push(psend.at[q, 3, hi], zr1.at[q, 1], z1_sem.at[2 * q + 1], dp_prev)
    turn_x(SIDE - 1, 0)

    def merge(q):
        arrive(zr1.at[q, 0], z1_sem.at[2 * q])
        psend[q, 2, lo] = (psend[q, 2, lo].astype(F32) + zr1[q, 0].astype(F32)).astype(BF16)
        push(psend.at[q, 2, lo], zr2.at[q, 0, lo], z2_sem.at[4 * q + 2], dp_next)
        arrive(zr1.at[q, 1], z1_sem.at[2 * q + 1])
        psend[q, 1, hi] = (psend[q, 1, hi].astype(F32) + zr1[q, 1].astype(F32)).astype(BF16)
        push(psend.at[q, 1, hi], zr2.at[q, 1, hi], z2_sem.at[4 * q + 3], dp_prev)

    def slab(h, s):
        for i in range(SIDE):
            lhs[pl.ds(i * rows, rows), :] = xt[h, flat(h, i, s)]
        return jnp.dot(lhs[...], pg[...], preferred_element_type=F32).reshape(SIDE, rows, width)

    for n, i in enumerate((2, 1, 3, 0)):
        s = m4(a + i)
        ssend[s] = slab(1 - k, s).astype(BF16)
        push(ssend.at[s], srecv.at[s], s_sem.at[n], sibling)

    one, two = pl.ds(0, 2), pl.ds(2, 2)
    for n, i in enumerate((2, 1, 3, 0)):
        s = m4(b + i)
        arrive(srecv.at[s], s_sem.at[n])
        dsend[s] = (slab(k, s) + srecv[s].astype(F32)).astype(BF16)
        if i == 2:
            push(dsend.at[s, one], r1.at[0], r_sem.at[0], b_next)
            push(dsend.at[s, two], r1.at[1], r_sem.at[1], b_prev)
        if i == 1:
            push(dsend.at[s, two], r2.at[0, two], r_sem.at[2], b_next)
        if i == 3:
            push(dsend.at[s, one], r2.at[1, one], r_sem.at[3], b_prev)

    merge(0)
    s = m4(b + 1)
    arrive(r1.at[0], r_sem.at[0])
    dsend[s, one] = (dsend[s, one].astype(F32) + r1[0].astype(F32)).astype(BF16)
    push(dsend.at[s, one], r2.at[0, one], r_sem.at[8], b_next)
    s = m4(b + 3)
    arrive(r1.at[1], r_sem.at[1])
    dsend[s, two] = (dsend[s, two].astype(F32) + r1[1].astype(F32)).astype(BF16)
    push(dsend.at[s, two], r2.at[1, two], r_sem.at[9], b_prev)
    for q in range(1, quarters):
        merge(q)

    def turn_out(step, _):
        slot, j = lax.div(step, tiles), lax.rem(step, tiles)
        at = pl.ds(pl.multiple_of(j * TILE, TILE), TILE)
        block = outn[pl.ds(pl.multiple_of(slot * toks, toks), toks), at].astype(F32).T.astype(BF16)
        outt[clip_at(slot), at, :] = block
        return 0

    lax.fori_loop(0, SIDE * tiles, turn_out, 0)
    store_out = pltpu.make_async_copy(outt.at[:, pl.ds(0, units), :], out_hbm, local_sem.at[1])
    store_out.start()

    arrive(r2.at[0, two], r_sem.at[2])
    arrive(r2.at[1, one], r_sem.at[3])
    arrive(r2.at[0, one], r_sem.at[8])
    arrive(r2.at[1, two], r_sem.at[9])
    for i, to in ((2, a_far), (1, a_next), (3, a_prev), (0, None)):
        ai = m4(a + i)
        total = dsend[b, ai].astype(F32) + r2[0, ai].astype(F32) + r2[1, ai].astype(F32)
        dsend[b, ai] = total.astype(BF16)
        if to is not None:
            push(dsend.at[b, ai], r3.at[i - 1], r_sem.at[3 + i], to)

    for i in (1, 2, 3):
        arrive(r3.at[i - 1], r_sem.at[3 + i])

    def plane():
        return dsend[b, a].astype(F32) + r3[0].astype(F32) + r3[1].astype(F32) + r3[2].astype(F32)

    last = remote(d4, r4, send_sem.at[send_sem.shape[0] - 3], r_sem.at[7], across)
    back = remote(fin.at[1 - k], fin.at[1 - k], send_sem.at[send_sem.shape[0] - 4], s_sem.at[4], sibling)

    @pl.when(jnp.logical_not(home))
    def _():
        d4[...] = plane().astype(BF16)
        last.start()

    for q in range(quarters):
        arrive(zr2.at[q, 0, hi], z2_sem.at[4 * q])
        arrive(zr2.at[q, 1, lo], z2_sem.at[4 * q + 1])
        arrive(zr2.at[q, 0, lo], z2_sem.at[4 * q + 2])
        arrive(zr2.at[q, 1, hi], z2_sem.at[4 * q + 3])
        total = psend[q, 0].astype(F32) + zr2[q, 0].astype(F32) + zr2[q, 1].astype(F32)
        ing[:, pl.ds(q * quarter, quarter)] = total.astype(BF16)
    store_ing = pltpu.make_async_copy(ing, ing_hbm.at[0], local_sem.at[0])
    store_ing.start()

    @pl.when(home)
    def _():
        arrive(r4, r_sem.at[7])
        fin[...] = ((plane() + r4[...].astype(F32)) * factor).reshape(2, own_rows, width)
        back.start()
        back.wait_send()

    @pl.when(jnp.logical_not(home))
    def _():
        last.wait_send()
        arrive(fin.at[k], s_sem.at[4])

    dw_ref[...] = fin[k, :, pl.ds(0, units)]

    cross.wait_send()

    @pl.when(jnp.logical_not(home))
    def _():
        stage.wait_send()

    for copy in sends:
        copy.wait_send()
    store_out.wait()
    store_ing.wait()


def on_device(inputs, up_weight, out_grad):
    _, toks, depth = inputs.shape
    own_rows, units = up_weight.shape
    clips = out_grad.shape[0]
    rows = 2 * own_rows
    padded = -(-own_rows // 16) * 16
    chips = SIDE * SIDE
    width = -(-units // TILE) * TILE
    quarters = 4
    quarter = depth // quarters
    every = clips * toks
    factor = 1.0 / float(every * 4 * chips) ** 0.5

    out_t, in_grad, up_grad = pl.pallas_call(
        functools.partial(kernel, factor),
        out_shape=(
            jax.ShapeDtypeStruct((clips, units, toks), BF16),
            jax.ShapeDtypeStruct((1, toks, depth), BF16),
            jax.ShapeDtypeStruct((own_rows, units), F32),
        ),
        in_specs=[
            pl.BlockSpec(memory_space=pl.ANY),
            pl.BlockSpec(memory_space=pltpu.VMEM),
            pl.BlockSpec(memory_space=pl.ANY),
        ],
        out_specs=(
            pl.BlockSpec(memory_space=pl.ANY),
            pl.BlockSpec(memory_space=pl.ANY),
            pl.BlockSpec(memory_space=pltpu.VMEM),
        ),
        scratch_shapes=[
            pltpu.VMEM((clips, toks, depth), BF16),
            pltpu.VMEM((2, chips, rows, every), BF16),
            pltpu.VMEM((2, chips, rows, width), BF16),
            pltpu.VMEM((padded, width), BF16),
            pltpu.VMEM((2, padded, width), BF16),
            pltpu.VMEM((clips, width, toks), BF16),
            pltpu.VMEM((every, width), BF16),
            pltpu.VMEM((every, width), BF16),
            pltpu.VMEM((every, width), BF16),
            pltpu.VMEM((clips, width, toks), BF16),
            pltpu.VMEM((every, TILE), F32),
            pltpu.VMEM((quarters, clips, toks, quarter), BF16),
            pltpu.VMEM((quarters, 2, toks // 2, quarter), BF16),
            pltpu.VMEM((quarters, 2, toks, quarter), BF16),
            pltpu.VMEM((toks, depth), BF16),
            pltpu.VMEM((SIDE * rows, every), BF16),
            pltpu.VMEM((SIDE, SIDE, rows, width), BF16),
            pltpu.VMEM((SIDE, SIDE, rows, width), BF16),
            pltpu.VMEM((SIDE, SIDE, rows, width), BF16),
            pltpu.VMEM((2, 2, rows, width), BF16),
            pltpu.VMEM((2, SIDE, rows, width), BF16),
            pltpu.VMEM((3, rows, width), BF16),
            pltpu.VMEM((rows, width), BF16),
            pltpu.VMEM((rows, width), BF16),
            pltpu.VMEM((2, own_rows, width), F32),
            pltpu.SemaphoreType.DMA((96,)),
            pltpu.SemaphoreType.DMA((2 * chips,)),
            pltpu.SemaphoreType.DMA((2,)),
            pltpu.SemaphoreType.DMA((6,)),
            pltpu.SemaphoreType.DMA((2 * quarters,)),
            pltpu.SemaphoreType.DMA((4 * quarters,)),
            pltpu.SemaphoreType.DMA((6,)),
            pltpu.SemaphoreType.DMA((10,)),
            pltpu.SemaphoreType.DMA((2,)),
        ],
        compiler_params=pltpu.CompilerParams(
            collective_id=0, has_side_effects=True, vmem_limit_bytes=60 * 1024 * 1024
        ),
        cost_estimate=pl.CostEstimate(
            flops=6 * every * depth * units, bytes_accessed=6_000_000, transcendentals=every * units
        ),
    )(inputs, up_weight, out_grad.transpose(0, 2, 1))
    return out_t.transpose(0, 2, 1), in_grad, up_grad


def solution(mesh):
    in_specs = (P("dp", "fsdp", None), P("fsdp", "dp"), P(None, "fsdp", "dp"))
    out_specs = (P(None, "fsdp", "dp"), P("dp", "fsdp", None), P("fsdp", "dp"))
    return jax.shard_map(
        on_device, mesh=mesh, in_specs=in_specs, out_specs=out_specs, check_vma=False
    )
```

```python
import functools

import jax
import jax.numpy as jnp
from jax import lax
from jax.experimental import pallas as pl
from jax.experimental.pallas import tpu as pltpu
from jax.sharding import PartitionSpec as P

MESH = pl.DeviceIdType.MESH
F32, BF16 = jnp.float32, jnp.bfloat16
SIDE = 4
TILE = 256
CHUNK = 64


def place(device):
    return {"fsdp": device[0], "dp": device[1]}


def remote(src, dst, send_sem, recv_sem, device):
    return pltpu.make_async_remote_copy(
        src_ref=src, dst_ref=dst, send_sem=send_sem, recv_sem=recv_sem,
        device_id=place(device), device_id_type=MESH,
    )


def gelu_pair(v):
    c = 0.7978845608028654
    sq = v * v
    t = jnp.tanh(v * (c + (c * 0.044715) * sq))
    half = 0.5 * (1.0 + t)
    slope = half + (0.5 * v) * (1.0 - t * t) * (c + (3.0 * c * 0.044715) * sq)
    return v * half, slope


def kernel(
    factor, x_hbm, w_ref, gt_hbm, out_hbm, ing_hbm, dw_ref,
    xall, xt, wfull, wown, wst, gt, g, pg, outn, outt, pre, psend, zr1, zr2, ing,
    ssend, srecv, dsend, r1, r2, r3, d4, r4, fin,
    send_sem, w_sem, p_sem, x_sem, z1_sem, z2_sem, s_sem, r_sem, local_sem,
):
    fs, p = lax.axis_index("fsdp"), lax.axis_index("dp")
    k = lax.rem(fs, 2)
    x = lax.rem(lax.div(fs, 2), SIDE)
    y = lax.rem(lax.div(fs, 2 * SIDE), SIDE)
    l = lax.div(fs, 2 * SIDE * SIDE)
    home = k == l
    a = x * (1 - k) + y * k
    b = y * (1 - k) + x * k
    toks = xall.shape[1]
    half_toks = toks // 2
    near = (SIDE - 1) * toks
    rows = wfull.shape[2]
    own_rows = rows // 2
    width = wfull.shape[3]
    units = w_ref.shape[1]
    tiles = width // TILE
    quarter = psend.shape[3]
    quarters = psend.shape[0]
    blocks = quarter // rows

    def m4(v):
        return lax.rem(v, SIDE)

    def device(a_to, b_to):
        x_to = a_to * (1 - k) + b_to * k
        y_to = b_to * (1 - k) + a_to * k
        return (((l * SIDE + y_to) * SIDE + x_to) * 2 + k, p)

    def flat(h, a_at, b_at):
        return (a_at * (1 - h) + b_at * h) + SIDE * (b_at * (1 - h) + a_at * h)

    def clip_at(slot):
        return m4(p + jnp.where(slot == 0, 0, jnp.where(slot == 1, 3, slot - 1)))

    sibling = (fs + 1 - 2 * k, p)
    across = (fs + (1 - 2 * l) * (2 * SIDE * SIDE), p)
    askew = (across[0] + 1 - 2 * k, p)
    a_next, a_prev, a_far = (device(m4(a + i), b) for i in (1, 3, 2))
    b_next, b_prev = device(a, m4(b + 1)), device(a, m4(b + 3))
    dp_next, dp_prev = (fs, m4(p + 1)), (fs, m4(p + 3))

    sends = []

    def push(src, dst, recv_sem, to):
        copy = remote(src, dst, send_sem.at[len(sends)], recv_sem, to)
        sends.append(copy)
        copy.start()

    def arrive(dst, recv_sem):
        remote(dst, dst, send_sem.at[0], recv_sem, sibling).wait_recv()

    load_x = pltpu.make_async_copy(x_hbm.at[0], xall.at[0], local_sem.at[0])
    load_x.start()
    load_g = pltpu.make_async_copy(gt_hbm, gt.at[:, pl.ds(0, units), :], local_sem.at[1])
    load_g.start()

    barrier = pltpu.get_barrier_semaphore()
    peers = (sibling, across, askew, a_next, a_prev, a_far, b_next, b_prev, dp_next, dp_prev)
    for peer in peers:
        pl.semaphore_signal(barrier, inc=1, device_id=place(peer), device_id_type=MESH)

    spare = wown.shape[0] - own_rows
    wown[:, pl.ds(units, width - units)] = jnp.zeros((wown.shape[0], width - units), BF16)
    wown[:, pl.ds(0, units)] = jnp.concatenate([w_ref[...].astype(F32), jnp.zeros((spare, units), F32)], axis=0).astype(BF16)

    @pl.when(home)
    def _():
        wst[k] = wown[...]

    gt[:, pl.ds(units, width - units), :] = jnp.zeros((SIDE, width - units, toks), BF16)
    load_x.wait()
    pl.semaphore_wait(barrier, len(peers))

    mine = flat(k, a, b)

    def wblock(h, at):
        return wfull.at[h, at]

    def wsem(h, at):
        return w_sem.at[h * (SIDE * SIDE) + at]

    stage = remote(wown, wst.at[k], send_sem.at[send_sem.shape[0] - 1], p_sem.at[k], sibling)
    cross = remote(wown, wst.at[k], send_sem.at[send_sem.shape[0] - 2], p_sem.at[k], (across[0] + l - k, p))
    cross.start()

    @pl.when(jnp.logical_not(home))
    def _():
        stage.start()

    arrive(wst.at[1 - k], p_sem.at[1 - k])

    @pl.when(jnp.logical_not(home))
    def _():
        arrive(wst.at[k], p_sem.at[k])

    lo, hi = pl.ds(0, half_toks), pl.ds(half_toks, half_toks)
    push(xall.at[0, lo], xall.at[1, lo], x_sem.at[0], dp_next)
    push(xall.at[0, hi], xall.at[2, hi], x_sem.at[2], dp_prev)

    wfull[k, mine] = wst[...].astype(F32)[:, :own_rows].reshape(rows, width).astype(BF16)

    def share(at, *devices):
        for to in devices:
            push(wblock(k, at), wblock(k, at), wsem(k, at), to)

    order = (0, 1, 3, 2)
    by_next = (0, 3)
    share(mine, a_next, a_prev, a_far, b_next, b_prev, sibling)

    load_g.wait()

    def turn_g(step, _):
        slot, j = lax.div(step, tiles), lax.rem(step, tiles)
        at = pl.ds(pl.multiple_of(j * TILE, TILE), TILE)
        block = gt[clip_at(slot), at, :].astype(F32).T.astype(BF16)
        g[pl.ds(pl.multiple_of(slot * toks, toks), toks), at] = block
        return 0

    lax.fori_loop(0, SIDE * tiles, turn_g, 0)

    push(xall.at[0, hi], xall.at[1, hi], x_sem.at[1], dp_next)
    push(xall.at[0, lo], xall.at[2, lo], x_sem.at[3], dp_prev)
    for i in order[1:]:
        at = flat(k, m4(a + i), b)
        arrive(wblock(k, at), wsem(k, at))
        share(at, b_next, b_prev, sibling)

    for i in order:
        at = flat(k, m4(a + i), m4(b + 3))
        arrive(wblock(k, at), wsem(k, at))
        share(at, *((b_next, sibling) if i in by_next else (sibling,)))
        at = flat(k, m4(a + i), m4(b + 1))
        arrive(wblock(k, at), wsem(k, at))
        share(at, *((sibling,) if i in by_next else (b_prev, sibling)))

    arrive(xall.at[1, lo], x_sem.at[0])
    push(xall.at[1, lo], xall.at[3, lo], x_sem.at[4], dp_next)
    arrive(xall.at[2, hi], x_sem.at[2])
    push(xall.at[2, hi], xall.at[3, hi], x_sem.at[5], dp_prev)

    def turn_x(slot):
        at = pl.ds(slot * toks, toks)
        for q in range(quarters):
            block = xall[slot, :, pl.ds(q * quarter, quarter)].astype(F32).T.astype(BF16).reshape(blocks, rows, toks)
            for i in range(blocks):
                h, chip = divmod(q * blocks + i, SIDE * SIDE)
                y_at, x_at = divmod(chip, SIDE)
                first, second = (x_at, y_at) if h == 0 else (y_at, x_at)
                xt[h, second, first, :, at] = block[i]

    for i in order:
        at = flat(k, m4(a + i), m4(b + 2))
        arrive(wblock(k, at), wsem(k, at))
        share(at, sibling)
    arrive(xall.at[1, hi], x_sem.at[1])
    arrive(xall.at[2, lo], x_sem.at[3])
    for slot in range(SIDE - 1):
        turn_x(slot)
    for at in range(SIDE * SIDE):
        arrive(wblock(1 - k, at), wsem(1 - k, at))

    def forward(first, count, start, stop):
        def tile(j, _):
            at = pl.ds(pl.multiple_of(j * TILE, TILE), TILE)
            pre[pl.ds(0, count * toks), :] = jnp.dot(
                xall[pl.ds(first, count)].reshape(count * toks, -1),
                wfull[:, :, :, at].reshape(-1, TILE), preferred_element_type=F32,
            )

            def chunk(r, _):
                span = pl.ds(pl.multiple_of(r * CHUNK, CHUNK), CHUNK)
                to = pl.ds(pl.multiple_of(r * CHUNK + first * toks, CHUNK), CHUNK)
                value, slope = gelu_pair(pre[span, :])
                outn[to, at] = value.astype(BF16)
                pg[to, at] = (g[to, at].astype(F32) * slope).astype(BF16)
                return 0

            lax.fori_loop(0, count * toks // CHUNK, chunk, 0)
            return 0

        lax.fori_loop(start, stop, tile, 0)

    def in_grad_part(q, first, count):
        start = q * blocks
        h, at = start // (SIDE * SIDE), start % (SIDE * SIDE)
        wq = wfull[h, pl.ds(at, blocks)].reshape(quarter, width)
        part = lax.dot_general(
            pg[pl.ds(first * toks, count * toks), :], wq, (((1,), (1,)), ((), ())), preferred_element_type=F32
        )
        psend[q, pl.ds(first, count)] = part.astype(BF16).reshape(count, toks, quarter)

    forward(0, SIDE - 1, 0, tiles)

    for q in range(quarters):
        in_grad_part(q, 0, SIDE - 1)
        push(psend.at[q, 2, hi], zr2.at[q, 0, hi], z2_sem.at[4 * q], dp_next)
        push(psend.at[q, 1, lo], zr2.at[q, 1, lo], z2_sem.at[4 * q + 1], dp_prev)

    one, two = pl.ds(0, 2), pl.ds(2, 2)
    starts = [sum(d.shape[3] for d in dsend[:c]) for c in range(len(dsend))]

    def slab(c, h, s):
        at = pl.ds(starts[c], dsend[c].shape[3])
        left = xt[h, s].reshape(SIDE * rows, SIDE * toks)
        return jnp.dot(left, pg[:, at], preferred_element_type=F32).reshape(SIDE, rows, -1)

    def slabs(c):
        for n, i in enumerate((2, 1, 3, 0)):
            s = m4(a + i)
            ssend[c][s] = slab(c, 1 - k, s).astype(BF16)
            push(ssend[c].at[s], srecv[c].at[s], s_sem.at[SIDE * c + n], sibling)
        for n, i in enumerate((2, 1, 3, 0)):
            s = m4(b + i)
            arrive(srecv[c].at[s], s_sem.at[SIDE * c + n])
            dsend[c][s] = (slab(c, k, s) + srecv[c][s].astype(F32)).astype(BF16)
            if i == 2:
                push(dsend[c].at[s, one], r1[c].at[0], r_sem.at[c, 0], b_next)
                push(dsend[c].at[s, two], r1[c].at[1], r_sem.at[c, 1], b_prev)
            if i == 1:
                push(dsend[c].at[s, two], r2[c].at[0, two], r_sem.at[c, 2], b_next)
            if i == 3:
                push(dsend[c].at[s, one], r2[c].at[1, one], r_sem.at[c, 3], b_prev)

    def pass_on(c):
        s = m4(b + 1)
        arrive(r1[c].at[0], r_sem.at[c, 0])
        dsend[c][s, one] = (dsend[c][s, one].astype(F32) + r1[c][0].astype(F32)).astype(BF16)
        push(dsend[c].at[s, one], r2[c].at[0, one], r_sem.at[c, 8], b_next)
        s = m4(b + 3)
        arrive(r1[c].at[1], r_sem.at[c, 1])
        dsend[c][s, two] = (dsend[c][s, two].astype(F32) + r1[c][1].astype(F32)).astype(BF16)
        push(dsend[c].at[s, two], r2[c].at[1, two], r_sem.at[c, 9], b_prev)

    def along_first(c):
        arrive(r2[c].at[0, two], r_sem.at[c, 2])
        arrive(r2[c].at[1, one], r_sem.at[c, 3])
        arrive(r2[c].at[0, one], r_sem.at[c, 8])
        arrive(r2[c].at[1, two], r_sem.at[c, 9])
        for i, to in ((2, a_far), (1, a_next), (3, a_prev), (0, None)):
            ai = m4(a + i)
            total = dsend[c][b, ai].astype(F32) + r2[c][0, ai].astype(F32) + r2[c][1, ai].astype(F32)
            dsend[c][b, ai] = total.astype(BF16)
            if to is not None:
                push(dsend[c].at[b, ai], r3[c].at[i - 1], r_sem.at[c, 3 + i], to)

    def plane(c):
        return dsend[c][b, a].astype(F32) + r3[c][0].astype(F32) + r3[c][1].astype(F32) + r3[c][2].astype(F32)

    last = [
        remote(d4[c], r4[c], send_sem.at[send_sem.shape[0] - 4 - c], r_sem.at[c, 7], across) for c in range(len(d4))
    ]
    back = remote(fin.at[1 - k], fin.at[1 - k], send_sem.at[send_sem.shape[0] - 3], s_sem.at[s_sem.shape[0] - 1], sibling)

    def across_planes(c):
        for i in (1, 2, 3):
            arrive(r3[c].at[i - 1], r_sem.at[c, 3 + i])

        @pl.when(jnp.logical_not(home))
        def _():
            d4[c][...] = plane(c).astype(BF16)
            last[c].start()

    def merge(q):
        arrive(zr1.at[q, 0], z1_sem.at[2 * q])
        psend[q, 2, lo] = (psend[q, 2, lo].astype(F32) + zr1[q, 0].astype(F32)).astype(BF16)
        push(psend.at[q, 2, lo], zr2.at[q, 0, lo], z2_sem.at[4 * q + 2], dp_next)
        arrive(zr1.at[q, 1], z1_sem.at[2 * q + 1])
        psend[q, 1, hi] = (psend[q, 1, hi].astype(F32) + zr1[q, 1].astype(F32)).astype(BF16)
        push(psend.at[q, 1, hi], zr2.at[q, 1, hi], z2_sem.at[4 * q + 3], dp_prev)

    arrive(xall.at[3, lo], x_sem.at[4])
    arrive(xall.at[3, hi], x_sem.at[5])
    turn_x(SIDE - 1)
    forward(SIDE - 1, 1, 0, starts[1] // TILE)
    slabs(0)
    forward(SIDE - 1, 1, starts[1] // TILE, tiles)
    pass_on(0)

    for q in range(quarters):
        in_grad_part(q, SIDE - 1, 1)
        push(psend.at[q, 3, lo], zr1.at[q, 0], z1_sem.at[2 * q], dp_next)
        push(psend.at[q, 3, hi], zr1.at[q, 1], z1_sem.at[2 * q + 1], dp_prev)

    slabs(1)
    along_first(0)
    pass_on(1)
    merge(0)
    merge(1)
    across_planes(0)
    merge(2)
    merge(3)

    def turn_out(step, _):
        slot, j = lax.div(step, tiles), lax.rem(step, tiles)
        at = pl.ds(pl.multiple_of(j * TILE, TILE), TILE)
        block = outn[pl.ds(pl.multiple_of(slot * toks, toks), toks), at].astype(F32).T.astype(BF16)
        outt[clip_at(slot), at, :] = block
        return 0

    along_first(1)
    lax.fori_loop(0, SIDE * tiles, turn_out, 0)
    store_out = pltpu.make_async_copy(outt.at[:, pl.ds(0, units), :], out_hbm, local_sem.at[1])
    store_out.start()
    across_planes(1)

    for q in range(quarters):
        arrive(zr2.at[q, 0, hi], z2_sem.at[4 * q])
        arrive(zr2.at[q, 1, lo], z2_sem.at[4 * q + 1])
        arrive(zr2.at[q, 0, lo], z2_sem.at[4 * q + 2])
        arrive(zr2.at[q, 1, hi], z2_sem.at[4 * q + 3])
        total = psend[q, 0].astype(F32) + zr2[q, 0].astype(F32) + zr2[q, 1].astype(F32)
        ing[:, pl.ds(q * quarter, quarter)] = total.astype(BF16)
    store_ing = pltpu.make_async_copy(ing, ing_hbm.at[0], local_sem.at[0])
    store_ing.start()

    @pl.when(home)
    def _():
        for c in range(len(d4)):
            arrive(r4[c], r_sem.at[c, 7])
            whole = ((plane(c) + r4[c][...].astype(F32)) * factor).reshape(2, own_rows, -1)
            fin[:, :, pl.ds(starts[c], d4[c].shape[1])] = whole
        back.start()
        back.wait_send()

    @pl.when(jnp.logical_not(home))
    def _():
        for copy in last:
            copy.wait_send()
        arrive(fin.at[k], s_sem.at[s_sem.shape[0] - 1])

    dw_ref[...] = fin[k, :, pl.ds(0, units)]

    cross.wait_send()

    @pl.when(jnp.logical_not(home))
    def _():
        stage.wait_send()

    for copy in sends:
        copy.wait_send()
    store_out.wait()
    store_ing.wait()


def on_device(inputs, up_weight, out_grad):
    _, toks, depth = inputs.shape
    own_rows, units = up_weight.shape
    clips = out_grad.shape[0]
    rows = 2 * own_rows
    padded = -(-own_rows // 16) * 16
    chips = SIDE * SIDE
    width = -(-units // TILE) * TILE
    quarters = 4
    quarter = depth // quarters
    every = clips * toks
    factor = 1.0 / float(every * 4 * chips) ** 0.5

    first_chunk = width // TILE // 2 * TILE

    def per_chunk(*lead):
        return tuple(pltpu.VMEM((*lead, columns), BF16) for columns in (first_chunk, width - first_chunk))

    out_t, in_grad, up_grad = pl.pallas_call(
        functools.partial(kernel, factor),
        out_shape=(
            jax.ShapeDtypeStruct((clips, units, toks), BF16),
            jax.ShapeDtypeStruct((1, toks, depth), BF16),
            jax.ShapeDtypeStruct((own_rows, units), F32),
        ),
        in_specs=[
            pl.BlockSpec(memory_space=pl.ANY),
            pl.BlockSpec(memory_space=pltpu.VMEM),
            pl.BlockSpec(memory_space=pl.ANY),
        ],
        out_specs=(
            pl.BlockSpec(memory_space=pl.ANY),
            pl.BlockSpec(memory_space=pl.ANY),
            pl.BlockSpec(memory_space=pltpu.VMEM),
        ),
        scratch_shapes=[
            pltpu.VMEM((clips, toks, depth), BF16),
            pltpu.VMEM((2, SIDE, SIDE, rows, every), BF16),
            pltpu.VMEM((2, chips, rows, width), BF16),
            pltpu.VMEM((padded, width), BF16),
            pltpu.VMEM((2, padded, width), BF16),
            pltpu.VMEM((clips, width, toks), BF16),
            pltpu.VMEM((every, width), BF16),
            pltpu.VMEM((every, width), BF16),
            pltpu.VMEM((every, width), BF16),
            pltpu.VMEM((clips, width, toks), BF16),
            pltpu.VMEM((every, TILE), F32),
            pltpu.VMEM((quarters, clips, toks, quarter), BF16),
            pltpu.VMEM((quarters, 2, toks // 2, quarter), BF16),
            pltpu.VMEM((quarters, 2, toks, quarter), BF16),
            pltpu.VMEM((toks, depth), BF16),
            per_chunk(SIDE, SIDE, rows),
            per_chunk(SIDE, SIDE, rows),
            per_chunk(SIDE, SIDE, rows),
            per_chunk(2, 2, rows),
            per_chunk(2, SIDE, rows),
            per_chunk(3, rows),
            per_chunk(rows),
            per_chunk(rows),
            pltpu.VMEM((2, own_rows, width), F32),
            pltpu.SemaphoreType.DMA((112,)),
            pltpu.SemaphoreType.DMA((2 * chips,)),
            pltpu.SemaphoreType.DMA((2,)),
            pltpu.SemaphoreType.DMA((6,)),
            pltpu.SemaphoreType.DMA((2 * quarters,)),
            pltpu.SemaphoreType.DMA((4 * quarters,)),
            pltpu.SemaphoreType.DMA((2 * SIDE + 1,)),
            pltpu.SemaphoreType.DMA((2, 10)),
            pltpu.SemaphoreType.DMA((2,)),
        ],
        compiler_params=pltpu.CompilerParams(
            collective_id=0, has_side_effects=True, vmem_limit_bytes=60 * 1024 * 1024
        ),
        cost_estimate=pl.CostEstimate(
            flops=6 * every * depth * units, bytes_accessed=6_000_000, transcendentals=every * units
        ),
    )(inputs, up_weight, out_grad.transpose(0, 2, 1))
    return out_t.transpose(0, 2, 1), in_grad, up_grad


def solution(mesh):
    in_specs = (P("dp", "fsdp", None), P("fsdp", "dp"), P(None, "fsdp", "dp"))
    out_specs = (P(None, "fsdp", "dp"), P("dp", "fsdp", None), P("fsdp", "dp"))
    return jax.shard_map(
        on_device, mesh=mesh, in_specs=in_specs, out_specs=out_specs, check_vma=False
    )
```

```python
import functools

import jax
import jax.numpy as jnp
from jax import lax
from jax.experimental import pallas as pl
from jax.experimental.pallas import tpu as pltpu
from jax.sharding import PartitionSpec as P

MESH = pl.DeviceIdType.MESH
F32, BF16 = jnp.float32, jnp.bfloat16
SIDE = 4
TILE = 256
CHUNK = 64


def place(device):
    return {"fsdp": device[0], "dp": device[1]}


def remote(src, dst, send_sem, recv_sem, device):
    return pltpu.make_async_remote_copy(
        src_ref=src, dst_ref=dst, send_sem=send_sem, recv_sem=recv_sem,
        device_id=place(device), device_id_type=MESH,
    )


def gelu_pair(v):
    c = 0.7978845608028654
    sq = v * v
    t = jnp.tanh(v * (c + (c * 0.044715) * sq))
    half = 0.5 * (1.0 + t)
    slope = half + (0.5 * v) * (1.0 - t * t) * (c + (3.0 * c * 0.044715) * sq)
    return v * half, slope


def kernel(
    factor, x_hbm, w_ref, gt_hbm, out_hbm, ing_hbm, dw_ref,
    xall, xt, wfull, wown, wst, gt, g, pg, outn, outt, pre, psend, zr1, zr2, ing,
    ssend, srecv, dsend, r1, r2, r3, d4, r4, fin,
    send_sem, w_sem, p_sem, x_sem, z1_sem, z2_sem, s_sem, r_sem, local_sem,
):
    fs, p = lax.axis_index("fsdp"), lax.axis_index("dp")
    k = lax.rem(fs, 2)
    x = lax.rem(lax.div(fs, 2), SIDE)
    y = lax.rem(lax.div(fs, 2 * SIDE), SIDE)
    l = lax.div(fs, 2 * SIDE * SIDE)
    home = k == l
    a = x * (1 - k) + y * k
    b = y * (1 - k) + x * k
    toks = xall.shape[1]
    half_toks = toks // 2
    near = (SIDE - 1) * toks
    rows = wfull.shape[2]
    own_rows = rows // 2
    width = wfull.shape[3]
    units = w_ref.shape[1]
    tiles = width // TILE
    quarter = psend.shape[3]
    quarters = psend.shape[0]
    blocks = quarter // rows

    def m4(v):
        return lax.rem(v, SIDE)

    def device(a_to, b_to):
        x_to = a_to * (1 - k) + b_to * k
        y_to = b_to * (1 - k) + a_to * k
        return (((l * SIDE + y_to) * SIDE + x_to) * 2 + k, p)

    def flat(h, a_at, b_at):
        return (a_at * (1 - h) + b_at * h) + SIDE * (b_at * (1 - h) + a_at * h)

    def clip_at(slot):
        return m4(p + jnp.where(slot == 0, 0, jnp.where(slot == 1, 3, slot - 1)))

    sibling = (fs + 1 - 2 * k, p)
    across = (fs + (1 - 2 * l) * (2 * SIDE * SIDE), p)
    askew = (across[0] + 1 - 2 * k, p)
    a_next, a_prev, a_far = (device(m4(a + i), b) for i in (1, 3, 2))
    b_next, b_prev = device(a, m4(b + 1)), device(a, m4(b + 3))
    dp_next, dp_prev = (fs, m4(p + 1)), (fs, m4(p + 3))

    sends = []

    def push(src, dst, recv_sem, to):
        copy = remote(src, dst, send_sem.at[len(sends)], recv_sem, to)
        sends.append(copy)
        copy.start()

    def arrive(dst, recv_sem):
        remote(dst, dst, send_sem.at[0], recv_sem, sibling).wait_recv()

    load_x = pltpu.make_async_copy(x_hbm.at[0], xall.at[0], local_sem.at[0])
    load_x.start()
    load_g = pltpu.make_async_copy(gt_hbm, gt.at[:, pl.ds(0, units), :], local_sem.at[1])
    load_g.start()

    barrier = pltpu.get_barrier_semaphore()
    peers = (sibling, across, askew, a_next, a_prev, a_far, b_next, b_prev, dp_next, dp_prev)
    for peer in peers:
        pl.semaphore_signal(barrier, inc=1, device_id=place(peer), device_id_type=MESH)

    spare = wown.shape[0] - own_rows
    wown[:, pl.ds(units, width - units)] = jnp.zeros((wown.shape[0], width - units), BF16)
    wown[:, pl.ds(0, units)] = jnp.concatenate([w_ref[...].astype(F32), jnp.zeros((spare, units), F32)], axis=0).astype(BF16)

    @pl.when(home)
    def _():
        wst[k] = wown[...]

    gt[:, pl.ds(units, width - units), :] = jnp.zeros((SIDE, width - units, toks), BF16)
    load_x.wait()
    pl.semaphore_wait(barrier, len(peers))

    mine = flat(k, a, b)

    def wblock(h, at):
        return wfull.at[h, at]

    def wsem(h, at):
        return w_sem.at[h * (SIDE * SIDE) + at]

    stage = remote(wown, wst.at[k], send_sem.at[send_sem.shape[0] - 1], p_sem.at[k], sibling)
    cross = remote(wown, wst.at[k], send_sem.at[send_sem.shape[0] - 2], p_sem.at[k], (across[0] + l - k, p))
    cross.start()

    @pl.when(jnp.logical_not(home))
    def _():
        stage.start()

    arrive(wst.at[1 - k], p_sem.at[1 - k])

    @pl.when(jnp.logical_not(home))
    def _():
        arrive(wst.at[k], p_sem.at[k])

    lo, hi = pl.ds(0, half_toks), pl.ds(half_toks, half_toks)
    push(xall.at[0, lo], xall.at[1, lo], x_sem.at[0], dp_next)
    push(xall.at[0, hi], xall.at[2, hi], x_sem.at[2], dp_prev)

    wfull[k, mine] = wst[...].astype(F32)[:, :own_rows].reshape(rows, width).astype(BF16)

    def share(at, *devices):
        for to in devices:
            push(wblock(k, at), wblock(k, at), wsem(k, at), to)

    order = (0, 1, 3, 2)
    by_next = (0, 3)
    share(mine, a_next, a_prev, a_far, b_next, b_prev, sibling)

    load_g.wait()

    def turn_g(step, _):
        slot, j = lax.div(step, tiles), lax.rem(step, tiles)
        at = pl.ds(pl.multiple_of(j * TILE, TILE), TILE)
        block = gt[clip_at(slot), at, :].astype(F32).T.astype(BF16)
        g[pl.ds(pl.multiple_of(slot * toks, toks), toks), at] = block
        return 0

    lax.fori_loop(0, SIDE * tiles, turn_g, 0)

    push(xall.at[0, hi], xall.at[1, hi], x_sem.at[1], dp_next)
    push(xall.at[0, lo], xall.at[2, lo], x_sem.at[3], dp_prev)
    for i in order[1:]:
        at = flat(k, m4(a + i), b)
        arrive(wblock(k, at), wsem(k, at))
        share(at, b_next, b_prev, sibling)

    for i in order:
        at = flat(k, m4(a + i), m4(b + 3))
        arrive(wblock(k, at), wsem(k, at))
        share(at, *((b_next, sibling) if i in by_next else (sibling,)))
        at = flat(k, m4(a + i), m4(b + 1))
        arrive(wblock(k, at), wsem(k, at))
        share(at, *((sibling,) if i in by_next else (b_prev, sibling)))

    arrive(xall.at[1, lo], x_sem.at[0])
    push(xall.at[1, lo], xall.at[3, lo], x_sem.at[4], dp_next)
    arrive(xall.at[2, hi], x_sem.at[2])
    push(xall.at[2, hi], xall.at[3, hi], x_sem.at[5], dp_prev)

    def turn_x(slot):
        at = pl.ds(slot * toks, toks)
        for q in range(quarters):
            block = xall[slot, :, pl.ds(q * quarter, quarter)].astype(F32).T.astype(BF16).reshape(blocks, rows, toks)
            for i in range(blocks):
                h, chip = divmod(q * blocks + i, SIDE * SIDE)
                y_at, x_at = divmod(chip, SIDE)
                first, second = (x_at, y_at) if h == 0 else (y_at, x_at)
                xt[h, second, first, :, at] = block[i]

    for i in order:
        at = flat(k, m4(a + i), m4(b + 2))
        arrive(wblock(k, at), wsem(k, at))
        share(at, sibling)
    arrive(xall.at[1, hi], x_sem.at[1])
    arrive(xall.at[2, lo], x_sem.at[3])
    for slot in range(SIDE - 1):
        turn_x(slot)
    for at in range(SIDE * SIDE):
        arrive(wblock(1 - k, at), wsem(1 - k, at))

    def forward(first, count, start, stop):
        def product(j, slot):
            at = pl.ds(j * TILE, TILE)
            pre[slot, pl.ds(0, count * toks), :] = jnp.dot(
                xall[pl.ds(first, count)].reshape(count * toks, -1),
                wfull[:, :, :, at].reshape(-1, TILE), preferred_element_type=F32,
            )

        def activate(j, slot):
            at = pl.ds(j * TILE, TILE)
            for r in range(count * toks // CHUNK):
                to = pl.ds(r * CHUNK + first * toks, CHUNK)
                value, slope = gelu_pair(pre[slot, pl.ds(r * CHUNK, CHUNK), :])
                outn[to, at] = value.astype(BF16)
                pg[to, at] = (g[to, at].astype(F32) * slope).astype(BF16)

        for j in range(start, stop + 1):
            if j > start:
                activate(j - 1, (j - 1) % 2)
            if j < stop:
                product(j, j % 2)

    def in_grad_part(q, first, count):
        start = q * blocks
        h, at = start // (SIDE * SIDE), start % (SIDE * SIDE)
        wq = wfull[h, pl.ds(at, blocks)].reshape(quarter, width)
        part = lax.dot_general(
            pg[pl.ds(first * toks, count * toks), :], wq, (((1,), (1,)), ((), ())), preferred_element_type=F32
        )
        psend[q, pl.ds(first, count)] = part.astype(BF16).reshape(count, toks, quarter)

    forward(0, SIDE - 1, 0, tiles)

    for q in range(quarters):
        in_grad_part(q, 0, SIDE - 1)
        push(psend.at[q, 2, hi], zr2.at[q, 0, hi], z2_sem.at[4 * q], dp_next)
        push(psend.at[q, 1, lo], zr2.at[q, 1, lo], z2_sem.at[4 * q + 1], dp_prev)

    one, two = pl.ds(0, 2), pl.ds(2, 2)
    starts = [sum(d.shape[3] for d in dsend[:c]) for c in range(len(dsend))]

    def slab(c, h, s):
        at = pl.ds(starts[c], dsend[c].shape[3])
        left = xt[h, s].reshape(SIDE * rows, SIDE * toks)
        return jnp.dot(left, pg[:, at], preferred_element_type=F32).reshape(SIDE, rows, -1)

    def slabs(c):
        for n, i in enumerate((2, 1, 3, 0)):
            s = m4(a + i)
            ssend[c][s] = slab(c, 1 - k, s).astype(BF16)
            push(ssend[c].at[s], srecv[c].at[s], s_sem.at[SIDE * c + n], sibling)
        for n, i in enumerate((2, 1, 3, 0)):
            s = m4(b + i)
            arrive(srecv[c].at[s], s_sem.at[SIDE * c + n])
            dsend[c][s] = (slab(c, k, s) + srecv[c][s].astype(F32)).astype(BF16)
            if i == 2:
                push(dsend[c].at[s, one], r1[c].at[0], r_sem.at[c, 0], b_next)
                push(dsend[c].at[s, two], r1[c].at[1], r_sem.at[c, 1], b_prev)
            if i == 1:
                push(dsend[c].at[s, two], r2[c].at[0, two], r_sem.at[c, 2], b_next)
            if i == 3:
                push(dsend[c].at[s, one], r2[c].at[1, one], r_sem.at[c, 3], b_prev)

    def pass_on(c):
        s = m4(b + 1)
        arrive(r1[c].at[0], r_sem.at[c, 0])
        dsend[c][s, one] = (dsend[c][s, one].astype(F32) + r1[c][0].astype(F32)).astype(BF16)
        push(dsend[c].at[s, one], r2[c].at[0, one], r_sem.at[c, 8], b_next)
        s = m4(b + 3)
        arrive(r1[c].at[1], r_sem.at[c, 1])
        dsend[c][s, two] = (dsend[c][s, two].astype(F32) + r1[c][1].astype(F32)).astype(BF16)
        push(dsend[c].at[s, two], r2[c].at[1, two], r_sem.at[c, 9], b_prev)

    def along_first(c):
        arrive(r2[c].at[0, two], r_sem.at[c, 2])
        arrive(r2[c].at[1, one], r_sem.at[c, 3])
        arrive(r2[c].at[0, one], r_sem.at[c, 8])
        arrive(r2[c].at[1, two], r_sem.at[c, 9])
        for i, to in ((2, a_far), (1, a_next), (3, a_prev), (0, None)):
            ai = m4(a + i)
            total = dsend[c][b, ai].astype(F32) + r2[c][0, ai].astype(F32) + r2[c][1, ai].astype(F32)
            dsend[c][b, ai] = total.astype(BF16)
            if to is not None:
                push(dsend[c].at[b, ai], r3[c].at[i - 1], r_sem.at[c, 3 + i], to)

    def plane(c):
        return dsend[c][b, a].astype(F32) + r3[c][0].astype(F32) + r3[c][1].astype(F32) + r3[c][2].astype(F32)

    last = [
        remote(d4[c], r4[c], send_sem.at[send_sem.shape[0] - 4 - c], r_sem.at[c, 7], across) for c in range(len(d4))
    ]
    back = remote(fin.at[1 - k], fin.at[1 - k], send_sem.at[send_sem.shape[0] - 3], s_sem.at[s_sem.shape[0] - 1], sibling)

    def across_planes(c):
        for i in (1, 2, 3):
            arrive(r3[c].at[i - 1], r_sem.at[c, 3 + i])

        @pl.when(jnp.logical_not(home))
        def _():
            d4[c][...] = plane(c).astype(BF16)
            last[c].start()

    def merge(q):
        arrive(zr1.at[q, 0], z1_sem.at[2 * q])
        psend[q, 2, lo] = (psend[q, 2, lo].astype(F32) + zr1[q, 0].astype(F32)).astype(BF16)
        push(psend.at[q, 2, lo], zr2.at[q, 0, lo], z2_sem.at[4 * q + 2], dp_next)
        arrive(zr1.at[q, 1], z1_sem.at[2 * q + 1])
        psend[q, 1, hi] = (psend[q, 1, hi].astype(F32) + zr1[q, 1].astype(F32)).astype(BF16)
        push(psend.at[q, 1, hi], zr2.at[q, 1, hi], z2_sem.at[4 * q + 3], dp_prev)

    arrive(xall.at[3, lo], x_sem.at[4])
    arrive(xall.at[3, hi], x_sem.at[5])
    turn_x(SIDE - 1)
    forward(SIDE - 1, 1, 0, starts[1] // TILE)
    slabs(0)
    forward(SIDE - 1, 1, starts[1] // TILE, tiles)
    pass_on(0)

    for q in range(quarters):
        in_grad_part(q, SIDE - 1, 1)
        push(psend.at[q, 3, lo], zr1.at[q, 0], z1_sem.at[2 * q], dp_next)
        push(psend.at[q, 3, hi], zr1.at[q, 1], z1_sem.at[2 * q + 1], dp_prev)

    slabs(1)
    along_first(0)
    pass_on(1)
    merge(0)
    merge(1)
    across_planes(0)
    merge(2)
    merge(3)

    def turn_out(step, _):
        slot, j = lax.div(step, tiles), lax.rem(step, tiles)
        at = pl.ds(pl.multiple_of(j * TILE, TILE), TILE)
        block = outn[pl.ds(pl.multiple_of(slot * toks, toks), toks), at].astype(F32).T.astype(BF16)
        outt[clip_at(slot), at, :] = block
        return 0

    along_first(1)
    lax.fori_loop(0, SIDE * tiles, turn_out, 0)
    store_out = pltpu.make_async_copy(outt.at[:, pl.ds(0, units), :], out_hbm, local_sem.at[1])
    store_out.start()
    across_planes(1)

    for q in range(quarters):
        arrive(zr2.at[q, 0, hi], z2_sem.at[4 * q])
        arrive(zr2.at[q, 1, lo], z2_sem.at[4 * q + 1])
        arrive(zr2.at[q, 0, lo], z2_sem.at[4 * q + 2])
        arrive(zr2.at[q, 1, hi], z2_sem.at[4 * q + 3])
        total = psend[q, 0].astype(F32) + zr2[q, 0].astype(F32) + zr2[q, 1].astype(F32)
        ing[:, pl.ds(q * quarter, quarter)] = total.astype(BF16)
    store_ing = pltpu.make_async_copy(ing, ing_hbm.at[0], local_sem.at[0])
    store_ing.start()

    @pl.when(home)
    def _():
        for c in range(len(d4)):
            arrive(r4[c], r_sem.at[c, 7])
            whole = ((plane(c) + r4[c][...].astype(F32)) * factor).reshape(2, own_rows, -1)
            fin[:, :, pl.ds(starts[c], d4[c].shape[1])] = whole
        back.start()
        back.wait_send()

    @pl.when(jnp.logical_not(home))
    def _():
        for copy in last:
            copy.wait_send()
        arrive(fin.at[k], s_sem.at[s_sem.shape[0] - 1])

    dw_ref[...] = fin[k, :, pl.ds(0, units)]

    cross.wait_send()

    @pl.when(jnp.logical_not(home))
    def _():
        stage.wait_send()

    for copy in sends:
        copy.wait_send()
    store_out.wait()
    store_ing.wait()


def on_device(inputs, up_weight, out_grad):
    _, toks, depth = inputs.shape
    own_rows, units = up_weight.shape
    clips = out_grad.shape[0]
    rows = 2 * own_rows
    padded = -(-own_rows // 16) * 16
    chips = SIDE * SIDE
    width = -(-units // TILE) * TILE
    quarters = 4
    quarter = depth // quarters
    every = clips * toks
    factor = 1.0 / float(every * 4 * chips) ** 0.5

    first_chunk = width // TILE // 2 * TILE

    def per_chunk(*lead):
        return tuple(pltpu.VMEM((*lead, columns), BF16) for columns in (first_chunk, width - first_chunk))

    out_t, in_grad, up_grad = pl.pallas_call(
        functools.partial(kernel, factor),
        out_shape=(
            jax.ShapeDtypeStruct((clips, units, toks), BF16),
            jax.ShapeDtypeStruct((1, toks, depth), BF16),
            jax.ShapeDtypeStruct((own_rows, units), F32),
        ),
        in_specs=[
            pl.BlockSpec(memory_space=pl.ANY),
            pl.BlockSpec(memory_space=pltpu.VMEM),
            pl.BlockSpec(memory_space=pl.ANY),
        ],
        out_specs=(
            pl.BlockSpec(memory_space=pl.ANY),
            pl.BlockSpec(memory_space=pl.ANY),
            pl.BlockSpec(memory_space=pltpu.VMEM),
        ),
        scratch_shapes=[
            pltpu.VMEM((clips, toks, depth), BF16),
            pltpu.VMEM((2, SIDE, SIDE, rows, every), BF16),
            pltpu.VMEM((2, chips, rows, width), BF16),
            pltpu.VMEM((padded, width), BF16),
            pltpu.VMEM((2, padded, width), BF16),
            pltpu.VMEM((clips, width, toks), BF16),
            pltpu.VMEM((every, width), BF16),
            pltpu.VMEM((every, width), BF16),
            pltpu.VMEM((every, width), BF16),
            pltpu.VMEM((clips, width, toks), BF16),
            pltpu.VMEM((2, every, TILE), F32),
            pltpu.VMEM((quarters, clips, toks, quarter), BF16),
            pltpu.VMEM((quarters, 2, toks // 2, quarter), BF16),
            pltpu.VMEM((quarters, 2, toks, quarter), BF16),
            pltpu.VMEM((toks, depth), BF16),
            per_chunk(SIDE, SIDE, rows),
            per_chunk(SIDE, SIDE, rows),
            per_chunk(SIDE, SIDE, rows),
            per_chunk(2, 2, rows),
            per_chunk(2, SIDE, rows),
            per_chunk(3, rows),
            per_chunk(rows),
            per_chunk(rows),
            pltpu.VMEM((2, own_rows, width), F32),
            pltpu.SemaphoreType.DMA((112,)),
            pltpu.SemaphoreType.DMA((2 * chips,)),
            pltpu.SemaphoreType.DMA((2,)),
            pltpu.SemaphoreType.DMA((6,)),
            pltpu.SemaphoreType.DMA((2 * quarters,)),
            pltpu.SemaphoreType.DMA((4 * quarters,)),
            pltpu.SemaphoreType.DMA((2 * SIDE + 1,)),
            pltpu.SemaphoreType.DMA((2, 10)),
            pltpu.SemaphoreType.DMA((2,)),
        ],
        compiler_params=pltpu.CompilerParams(
            collective_id=0, has_side_effects=True, vmem_limit_bytes=60 * 1024 * 1024
        ),
        cost_estimate=pl.CostEstimate(
            flops=6 * every * depth * units, bytes_accessed=6_000_000, transcendentals=every * units
        ),
    )(inputs, up_weight, out_grad.transpose(0, 2, 1))
    return out_t.transpose(0, 2, 1), in_grad, up_grad


def solution(mesh):
    in_specs = (P("dp", "fsdp", None), P("fsdp", "dp"), P(None, "fsdp", "dp"))
    out_specs = (P(None, "fsdp", "dp"), P("dp", "fsdp", None), P("fsdp", "dp"))
    return jax.shard_map(
        on_device, mesh=mesh, in_specs=in_specs, out_specs=out_specs, check_vma=False
    )
```

```python
import functools

import jax
import jax.numpy as jnp
from jax import lax
from jax.experimental import pallas as pl
from jax.experimental.pallas import tpu as pltpu
from jax.sharding import PartitionSpec as P

MESH = pl.DeviceIdType.MESH
F32, BF16 = jnp.float32, jnp.bfloat16
SIDE = 4
TILE = 256
CHUNK = 64


def place(device):
    return {"fsdp": device[0], "dp": device[1]}


def remote(src, dst, send_sem, recv_sem, device):
    return pltpu.make_async_remote_copy(
        src_ref=src, dst_ref=dst, send_sem=send_sem, recv_sem=recv_sem,
        device_id=place(device), device_id_type=MESH,
    )


def gelu_pair(v):
    c = 0.7978845608028654
    sq = v * v
    t = jnp.tanh(v * (c + (c * 0.044715) * sq))
    half = 0.5 * (1.0 + t)
    slope = half + (0.5 * v) * (1.0 - t * t) * (c + (3.0 * c * 0.044715) * sq)
    return v * half, slope


def kernel(
    factor, x_hbm, w_ref, gt_hbm, out_hbm, ing_hbm, dw_ref,
    xall, xt, wfull, wown, wst, gt, g, pg, outn, outt, pre, psend, zr1, zr2, ing,
    ssend, srecv, dsend, r1, r2, r3, d4, r4, fin,
    send_sem, w_sem, p_sem, x_sem, z1_sem, z2_sem, s_sem, r_sem, local_sem,
):
    fs, p = lax.axis_index("fsdp"), lax.axis_index("dp")
    k = lax.rem(fs, 2)
    x = lax.rem(lax.div(fs, 2), SIDE)
    y = lax.rem(lax.div(fs, 2 * SIDE), SIDE)
    l = lax.div(fs, 2 * SIDE * SIDE)
    home = k == l
    a = x * (1 - k) + y * k
    b = y * (1 - k) + x * k
    toks = xall.shape[1]
    half_toks = toks // 2
    near = (SIDE - 1) * toks
    rows = wfull.shape[2]
    own_rows = rows // 2
    width = wfull.shape[3]
    units = w_ref.shape[1]
    tiles = width // TILE
    quarter = psend.shape[3]
    quarters = psend.shape[0]
    blocks = quarter // rows

    def m4(v):
        return lax.rem(v, SIDE)

    def device(a_to, b_to):
        x_to = a_to * (1 - k) + b_to * k
        y_to = b_to * (1 - k) + a_to * k
        return (((l * SIDE + y_to) * SIDE + x_to) * 2 + k, p)

    def flat(h, a_at, b_at):
        return (a_at * (1 - h) + b_at * h) + SIDE * (b_at * (1 - h) + a_at * h)

    def clip_at(slot):
        return m4(p + jnp.where(slot == 0, 0, jnp.where(slot == 1, 3, slot - 1)))

    sibling = (fs + 1 - 2 * k, p)
    across = (fs + (1 - 2 * l) * (2 * SIDE * SIDE), p)
    askew = (across[0] + 1 - 2 * k, p)
    a_next, a_prev, a_far = (device(m4(a + i), b) for i in (1, 3, 2))
    b_next, b_prev = device(a, m4(b + 1)), device(a, m4(b + 3))
    dp_next, dp_prev = (fs, m4(p + 1)), (fs, m4(p + 3))

    sends = []

    def push(src, dst, recv_sem, to):
        copy = remote(src, dst, send_sem.at[len(sends)], recv_sem, to)
        sends.append(copy)
        copy.start()

    def arrive(dst, recv_sem):
        remote(dst, dst, send_sem.at[0], recv_sem, sibling).wait_recv()

    load_x = pltpu.make_async_copy(x_hbm.at[0], xall.at[0], local_sem.at[0])
    load_x.start()
    load_g = pltpu.make_async_copy(gt_hbm, gt.at[:, pl.ds(0, units), :], local_sem.at[1])
    load_g.start()

    barrier = pltpu.get_barrier_semaphore()
    peers = (sibling, across, askew, a_next, a_prev, a_far, b_next, b_prev, dp_next, dp_prev)
    for peer in peers:
        pl.semaphore_signal(barrier, inc=1, device_id=place(peer), device_id_type=MESH)

    spare = wown.shape[0] - own_rows
    wown[:, pl.ds(units, width - units)] = jnp.zeros((wown.shape[0], width - units), BF16)
    wown[:, pl.ds(0, units)] = jnp.concatenate([w_ref[...].astype(F32), jnp.zeros((spare, units), F32)], axis=0).astype(BF16)

    @pl.when(home)
    def _():
        wst[k] = wown[...]

    gt[:, pl.ds(units, width - units), :] = jnp.zeros((SIDE, width - units, toks), BF16)
    load_x.wait()
    pl.semaphore_wait(barrier, len(peers))

    mine = flat(k, a, b)

    def wblock(h, at):
        return wfull.at[h, at]

    def wsem(h, at):
        return w_sem.at[h * (SIDE * SIDE) + at]

    stage = remote(wown, wst.at[k], send_sem.at[send_sem.shape[0] - 1], p_sem.at[k], sibling)
    cross = remote(wown, wst.at[k], send_sem.at[send_sem.shape[0] - 2], p_sem.at[k], (across[0] + l - k, p))
    cross.start()

    @pl.when(jnp.logical_not(home))
    def _():
        stage.start()

    arrive(wst.at[1 - k], p_sem.at[1 - k])

    @pl.when(jnp.logical_not(home))
    def _():
        arrive(wst.at[k], p_sem.at[k])

    lo, hi = pl.ds(0, half_toks), pl.ds(half_toks, half_toks)
    push(xall.at[0, lo], xall.at[1, lo], x_sem.at[0], dp_next)
    push(xall.at[0, hi], xall.at[2, hi], x_sem.at[2], dp_prev)

    wfull[k, mine] = wst[...].astype(F32)[:, :own_rows].reshape(rows, width).astype(BF16)

    def share(at, *devices):
        for to in devices:
            push(wblock(k, at), wblock(k, at), wsem(k, at), to)

    order = (0, 1, 3, 2)
    by_next = (0, 3)
    share(mine, a_next, a_prev, a_far, b_next, b_prev, sibling)

    load_g.wait()

    def turn_g(step, _):
        slot, j = lax.div(step, tiles), lax.rem(step, tiles)
        at = pl.ds(pl.multiple_of(j * TILE, TILE), TILE)
        block = gt[clip_at(slot), at, :].astype(F32).T.astype(BF16)
        g[pl.ds(pl.multiple_of(slot * toks, toks), toks), at] = block
        return 0

    lax.fori_loop(0, SIDE * tiles, turn_g, 0)

    push(xall.at[0, hi], xall.at[1, hi], x_sem.at[1], dp_next)
    push(xall.at[0, lo], xall.at[2, lo], x_sem.at[3], dp_prev)
    for i in order[1:]:
        at = flat(k, m4(a + i), b)
        arrive(wblock(k, at), wsem(k, at))
        share(at, b_next, b_prev, sibling)

    for i in order:
        at = flat(k, m4(a + i), m4(b + 3))
        arrive(wblock(k, at), wsem(k, at))
        share(at, *((b_next, sibling) if i in by_next else (sibling,)))
        at = flat(k, m4(a + i), m4(b + 1))
        arrive(wblock(k, at), wsem(k, at))
        share(at, *((sibling,) if i in by_next else (b_prev, sibling)))

    arrive(xall.at[1, lo], x_sem.at[0])
    push(xall.at[1, lo], xall.at[3, lo], x_sem.at[4], dp_next)
    arrive(xall.at[2, hi], x_sem.at[2])
    push(xall.at[2, hi], xall.at[3, hi], x_sem.at[5], dp_prev)

    def turn_x(slot):
        at = pl.ds(slot * toks, toks)
        for q in range(quarters):
            block = xall[slot, :, pl.ds(q * quarter, quarter)].astype(F32).T.astype(BF16).reshape(blocks, rows, toks)
            for i in range(blocks):
                h, chip = divmod(q * blocks + i, SIDE * SIDE)
                y_at, x_at = divmod(chip, SIDE)
                first, second = (x_at, y_at) if h == 0 else (y_at, x_at)
                xt[h, second, first, :, at] = block[i]

    for i in order:
        at = flat(k, m4(a + i), m4(b + 2))
        arrive(wblock(k, at), wsem(k, at))
        share(at, sibling)
    arrive(xall.at[1, hi], x_sem.at[1])
    arrive(xall.at[2, lo], x_sem.at[3])
    for slot in range(SIDE - 1):
        turn_x(slot)
    for at in range(SIDE * SIDE):
        arrive(wblock(1 - k, at), wsem(1 - k, at))

    def forward(first, count, start, stop):
        def product(j, slot):
            at = pl.ds(j * TILE, TILE)
            pre[slot, pl.ds(0, count * toks), :] = jnp.dot(
                xall[pl.ds(first, count)].reshape(count * toks, -1),
                wfull[:, :, :, at].reshape(-1, TILE), preferred_element_type=F32,
            )

        def activate(j, slot):
            at = pl.ds(j * TILE, TILE)
            for r in range(count * toks // CHUNK):
                to = pl.ds(r * CHUNK + first * toks, CHUNK)
                value, slope = gelu_pair(pre[slot, pl.ds(r * CHUNK, CHUNK), :])
                outn[to, at] = value.astype(BF16)
                pg[to, at] = (g[to, at].astype(F32) * slope).astype(BF16)

        for j in range(start, stop + 1):
            if j > start:
                activate(j - 1, (j - 1) % 2)
            if j < stop:
                product(j, j % 2)

    def in_grad_part(q, first, count):
        start = q * blocks
        h, at = start // (SIDE * SIDE), start % (SIDE * SIDE)
        wq = wfull[h, pl.ds(at, blocks)].reshape(quarter, width)
        part = lax.dot_general(
            pg[pl.ds(first * toks, count * toks), :], wq, (((1,), (1,)), ((), ())), preferred_element_type=F32
        )
        psend[q, pl.ds(first, count)] = part.astype(BF16).reshape(count, toks, quarter)

    forward(0, SIDE - 1, 0, tiles)

    for q in range(quarters):
        in_grad_part(q, 0, SIDE - 1)
        push(psend.at[q, 2, hi], zr2.at[q, 0, hi], z2_sem.at[4 * q], dp_next)
        push(psend.at[q, 1, lo], zr2.at[q, 1, lo], z2_sem.at[4 * q + 1], dp_prev)

    one, two = pl.ds(0, 2), pl.ds(2, 2)
    starts = [sum(d.shape[3] for d in dsend[:c]) for c in range(len(dsend))]

    def slab(c, h, s):
        at = pl.ds(starts[c], dsend[c].shape[3])
        left = xt[h, s].reshape(SIDE * rows, SIDE * toks)
        return jnp.dot(left, pg[:, at], preferred_element_type=F32).reshape(SIDE, rows, -1)

    def slabs(c):
        for n, i in enumerate((2, 1, 3, 0)):
            s = m4(a + i)
            ssend[c][s] = slab(c, 1 - k, s).astype(BF16)
            push(ssend[c].at[s], srecv[c].at[s], s_sem.at[SIDE * c + n], sibling)
        for n, i in enumerate((2, 1, 3, 0)):
            s = m4(b + i)
            arrive(srecv[c].at[s], s_sem.at[SIDE * c + n])
            dsend[c][s] = (slab(c, k, s) + srecv[c][s].astype(F32)).astype(BF16)
            if i == 2:
                push(dsend[c].at[s, one], r1[c].at[0], r_sem.at[c, 0], b_next)
                push(dsend[c].at[s, two], r1[c].at[1], r_sem.at[c, 1], b_prev)
            if i == 1:
                push(dsend[c].at[s, two], r2[c].at[0, two], r_sem.at[c, 2], b_next)
            if i == 3:
                push(dsend[c].at[s, one], r2[c].at[1, one], r_sem.at[c, 3], b_prev)

    def pass_on(c):
        s = m4(b + 1)
        arrive(r1[c].at[0], r_sem.at[c, 0])
        dsend[c][s, one] = (dsend[c][s, one].astype(F32) + r1[c][0].astype(F32)).astype(BF16)
        push(dsend[c].at[s, one], r2[c].at[0, one], r_sem.at[c, 8], b_next)
        s = m4(b + 3)
        arrive(r1[c].at[1], r_sem.at[c, 1])
        dsend[c][s, two] = (dsend[c][s, two].astype(F32) + r1[c][1].astype(F32)).astype(BF16)
        push(dsend[c].at[s, two], r2[c].at[1, two], r_sem.at[c, 9], b_prev)

    def along_first(c):
        arrive(r2[c].at[0, two], r_sem.at[c, 2])
        arrive(r2[c].at[1, one], r_sem.at[c, 3])
        arrive(r2[c].at[0, one], r_sem.at[c, 8])
        arrive(r2[c].at[1, two], r_sem.at[c, 9])
        for i, to in ((2, a_far), (1, a_next), (3, a_prev), (0, None)):
            ai = m4(a + i)
            total = dsend[c][b, ai].astype(F32) + r2[c][0, ai].astype(F32) + r2[c][1, ai].astype(F32)
            dsend[c][b, ai] = total.astype(BF16)
            if to is not None:
                push(dsend[c].at[b, ai], r3[c].at[i - 1], r_sem.at[c, 3 + i], to)

    def plane(c):
        return dsend[c][b, a].astype(F32) + r3[c][0].astype(F32) + r3[c][1].astype(F32) + r3[c][2].astype(F32)

    last = [
        remote(d4[c], r4[c], send_sem.at[send_sem.shape[0] - 4 - c], r_sem.at[c, 7], across) for c in range(len(d4))
    ]
    back = remote(fin.at[1 - k], fin.at[1 - k], send_sem.at[send_sem.shape[0] - 3], s_sem.at[s_sem.shape[0] - 1], sibling)

    def across_planes(c):
        for i in (1, 2, 3):
            arrive(r3[c].at[i - 1], r_sem.at[c, 3 + i])

        @pl.when(jnp.logical_not(home))
        def _():
            d4[c][...] = plane(c).astype(BF16)
            last[c].start()

        @pl.when(home)
        def _():
            fin[:, :, pl.ds(starts[c], d4[c].shape[1])] = plane(c).reshape(2, own_rows, -1)

    def merge(q):
        arrive(zr1.at[q, 0], z1_sem.at[2 * q])
        psend[q, 2, lo] = (psend[q, 2, lo].astype(F32) + zr1[q, 0].astype(F32)).astype(BF16)
        push(psend.at[q, 2, lo], zr2.at[q, 0, lo], z2_sem.at[4 * q + 2], dp_next)
        arrive(zr1.at[q, 1], z1_sem.at[2 * q + 1])
        psend[q, 1, hi] = (psend[q, 1, hi].astype(F32) + zr1[q, 1].astype(F32)).astype(BF16)
        push(psend.at[q, 1, hi], zr2.at[q, 1, hi], z2_sem.at[4 * q + 3], dp_prev)

    arrive(xall.at[3, lo], x_sem.at[4])
    arrive(xall.at[3, hi], x_sem.at[5])
    turn_x(SIDE - 1)
    forward(SIDE - 1, 1, 0, starts[1] // TILE)
    slabs(0)
    forward(SIDE - 1, 1, starts[1] // TILE, tiles)
    pass_on(0)

    for q in range(quarters):
        in_grad_part(q, SIDE - 1, 1)
        push(psend.at[q, 3, lo], zr1.at[q, 0], z1_sem.at[2 * q], dp_next)
        push(psend.at[q, 3, hi], zr1.at[q, 1], z1_sem.at[2 * q + 1], dp_prev)

    slabs(1)
    along_first(0)
    pass_on(1)
    merge(0)
    merge(1)
    across_planes(0)
    merge(2)
    merge(3)

    def turn_out(step, _):
        slot, j = lax.div(step, tiles), lax.rem(step, tiles)
        at = pl.ds(pl.multiple_of(j * TILE, TILE), TILE)
        block = outn[pl.ds(pl.multiple_of(slot * toks, toks), toks), at].astype(F32).T.astype(BF16)
        outt[clip_at(slot), at, :] = block
        return 0

    along_first(1)
    lax.fori_loop(0, SIDE * tiles, turn_out, 0)
    store_out = pltpu.make_async_copy(outt.at[:, pl.ds(0, units), :], out_hbm, local_sem.at[1])
    store_out.start()
    across_planes(1)

    for q in range(quarters):
        arrive(zr2.at[q, 0, hi], z2_sem.at[4 * q])
        arrive(zr2.at[q, 1, lo], z2_sem.at[4 * q + 1])
        arrive(zr2.at[q, 0, lo], z2_sem.at[4 * q + 2])
        arrive(zr2.at[q, 1, hi], z2_sem.at[4 * q + 3])
        total = psend[q, 0].astype(F32) + zr2[q, 0].astype(F32) + zr2[q, 1].astype(F32)
        ing[:, pl.ds(q * quarter, quarter)] = total.astype(BF16)
    store_ing = pltpu.make_async_copy(ing, ing_hbm.at[0], local_sem.at[0])
    store_ing.start()

    @pl.when(home)
    def _():
        for c in range(len(d4)):
            arrive(r4[c], r_sem.at[c, 7])
            at = pl.ds(starts[c], d4[c].shape[1])
            fin[:, :, at] = (fin[:, :, at] + r4[c][...].astype(F32).reshape(2, own_rows, -1)) * factor
        back.start()
        back.wait_send()

    @pl.when(jnp.logical_not(home))
    def _():
        for copy in last:
            copy.wait_send()
        arrive(fin.at[k], s_sem.at[s_sem.shape[0] - 1])

    dw_ref[...] = fin[k, :, pl.ds(0, units)]

    cross.wait_send()

    @pl.when(jnp.logical_not(home))
    def _():
        stage.wait_send()

    for copy in sends:
        copy.wait_send()
    store_out.wait()
    store_ing.wait()


def on_device(inputs, up_weight, out_grad):
    _, toks, depth = inputs.shape
    own_rows, units = up_weight.shape
    clips = out_grad.shape[0]
    rows = 2 * own_rows
    padded = -(-own_rows // 16) * 16
    chips = SIDE * SIDE
    width = -(-units // TILE) * TILE
    quarters = 4
    quarter = depth // quarters
    every = clips * toks
    factor = 1.0 / float(every * 4 * chips) ** 0.5

    first_chunk = width // TILE // 2 * TILE

    def per_chunk(*lead):
        return tuple(pltpu.VMEM((*lead, columns), BF16) for columns in (first_chunk, width - first_chunk))

    out_t, in_grad, up_grad = pl.pallas_call(
        functools.partial(kernel, factor),
        out_shape=(
            jax.ShapeDtypeStruct((clips, units, toks), BF16),
            jax.ShapeDtypeStruct((1, toks, depth), BF16),
            jax.ShapeDtypeStruct((own_rows, units), F32),
        ),
        in_specs=[
            pl.BlockSpec(memory_space=pl.ANY),
            pl.BlockSpec(memory_space=pltpu.VMEM),
            pl.BlockSpec(memory_space=pl.ANY),
        ],
        out_specs=(
            pl.BlockSpec(memory_space=pl.ANY),
            pl.BlockSpec(memory_space=pl.ANY),
            pl.BlockSpec(memory_space=pltpu.VMEM),
        ),
        scratch_shapes=[
            pltpu.VMEM((clips, toks, depth), BF16),
            pltpu.VMEM((2, SIDE, SIDE, rows, every), BF16),
            pltpu.VMEM((2, chips, rows, width), BF16),
            pltpu.VMEM((padded, width), BF16),
            pltpu.VMEM((2, padded, width), BF16),
            pltpu.VMEM((clips, width, toks), BF16),
            pltpu.VMEM((every, width), BF16),
            pltpu.VMEM((every, width), BF16),
            pltpu.VMEM((every, width), BF16),
            pltpu.VMEM((clips, width, toks), BF16),
            pltpu.VMEM((2, every, TILE), F32),
            pltpu.VMEM((quarters, clips, toks, quarter), BF16),
            pltpu.VMEM((quarters, 2, toks // 2, quarter), BF16),
            pltpu.VMEM((quarters, 2, toks, quarter), BF16),
            pltpu.VMEM((toks, depth), BF16),
            per_chunk(SIDE, SIDE, rows),
            per_chunk(SIDE, SIDE, rows),
            per_chunk(SIDE, SIDE, rows),
            per_chunk(2, 2, rows),
            per_chunk(2, SIDE, rows),
            per_chunk(3, rows),
            per_chunk(rows),
            per_chunk(rows),
            pltpu.VMEM((2, own_rows, width), F32),
            pltpu.SemaphoreType.DMA((112,)),
            pltpu.SemaphoreType.DMA((2 * chips,)),
            pltpu.SemaphoreType.DMA((2,)),
            pltpu.SemaphoreType.DMA((6,)),
            pltpu.SemaphoreType.DMA((2 * quarters,)),
            pltpu.SemaphoreType.DMA((4 * quarters,)),
            pltpu.SemaphoreType.DMA((2 * SIDE + 1,)),
            pltpu.SemaphoreType.DMA((2, 10)),
            pltpu.SemaphoreType.DMA((2,)),
        ],
        compiler_params=pltpu.CompilerParams(
            collective_id=0, has_side_effects=True, vmem_limit_bytes=60 * 1024 * 1024
        ),
        cost_estimate=pl.CostEstimate(
            flops=6 * every * depth * units, bytes_accessed=6_000_000, transcendentals=every * units
        ),
    )(inputs, up_weight, out_grad.transpose(0, 2, 1))
    return out_t.transpose(0, 2, 1), in_grad, up_grad


def solution(mesh):
    in_specs = (P("dp", "fsdp", None), P("fsdp", "dp"), P(None, "fsdp", "dp"))
    out_specs = (P(None, "fsdp", "dp"), P("dp", "fsdp", None), P("fsdp", "dp"))
    return jax.shard_map(
        on_device, mesh=mesh, in_specs=in_specs, out_specs=out_specs, check_vma=False
    )
```
